512 devices in a mesh: pts: 128 (over y, z, core), ch: 4 (over x).
Axes of the slice: x: 4, y: 4, z: 16, core: 2. Of those that a mesh axis runs over, the one named last changes fastest.
Arguments:
- raw_points: bfloat16 [393216, 128], P('pts'), may hold values from -36 to 36
- cell_ids: int32 [393216], P('pts'), may hold values from 0 to 2047, as said below
- row_counts: int32 [128], replicated, may hold values from 512 to 2048, as said below
- hilbert_position: int32 [128, 2048], P('pts'), may hold values from -1 to 131071, as said below
- z_position: int32 [131072], P('pts'), may hold values from 0 to 131071, as said below
- pool_weight: bfloat16 [128, 256], replicated, may hold values from -0.5 to 0.5
- qkv_weight: bfloat16 [3, 256, 256], P(None, None, 'ch')
- proj_weight: bfloat16 [256, 256], P(None, 'ch'), may hold values from -0.375 to 0.375
- fc1_weight: bfloat16 [256, 1024], P(None, 'ch'), may hold values from -0.375 to 0.375
- fc2_weight: bfloat16 [1024, 256], P('ch'), may hold values from -0.1875 to 0.1875
Outputs:
- returned: bfloat16 [131072, 256], P('pts', 'ch')
The draws below stay inside these ranges and needn't reach their ends.
Inputs may be any that keep to these rules, and one draw needn't show every extreme that they name: `row_counts`: each count is a multiple of 128; the counts sum to 131072; the largest is 2048 and the smallest is 512. `cell_ids`: on each device the ids never fall, start at 0, skip no id and end at that device's count minus 1. `hilbert_position`: entry l of device a is -1 exactly where l >= row_counts[a]; the other entries together are a permutation of the 131072 positions; device a's cells go to each device's block of 1024 Hilbert positions in equal numbers, row_counts[a] / 128. `z_position`: the inverse of the placement given by hilbert_position; each block of 1024 Hilbert positions sends exactly 8 of its cells to each block of 1024 Z indices.
All inputs are finite; a program needn't handle non-finite values.
Results may differ from the reference program's by a relative error of at most 0.014.
The reference program's roundings to bfloat16 on the way count: a program that leaves them out, or rounds other values in their place, can miss the bound.
Values may be sent and summed in bfloat16 or wider, within the bound.
A program may use at most 64 MiB of HBM per device.

```python
import jax
import jax.numpy as jnp
from jax import lax

C_IN = 128
C = 256
HEADS = 16
FFN = 1024
PATCH = 1024
HEAD_DIM = 16
ROWS = 1024
CELLS = 131072
KMAX = 2048
RAW_DEV = 3072
N_PTS = 128


def layout_tables(key):
    peer_count = N_PTS
    base_units = ROWS // N_PTS
    half_units = base_units // 2
    deltas = jax.random.randint(jax.random.fold_in(key, 102), ((peer_count - 3) // 2,), -half_units + 1, half_units)
    paired = jnp.stack([deltas, -deltas], axis=1).reshape(-1).astype(jnp.int32)
    leftover = jnp.zeros(((peer_count - 3) % 2,), jnp.int32)
    special = jnp.array([base_units, -half_units, -half_units], jnp.int32)
    shifts = jnp.concatenate([special, paired, leftover])
    shuffle = jax.random.permutation(jax.random.fold_in(key, 103), peer_count)
    unit_count = base_units + shifts[shuffle]
    counts = (unit_count * peer_count).astype(jnp.int32)
    gap_keys = jax.random.split(jax.random.fold_in(key, 104), peer_count)
    scores = jax.vmap(lambda sub_key: jax.random.permutation(sub_key, RAW_DEV - 1))(gap_keys)
    boundary = (scores < counts[:, None] - 1).astype(jnp.int32)
    cell_table = jnp.concatenate([jnp.zeros((peer_count, 1), jnp.int32), jnp.cumsum(boundary, axis=1).astype(jnp.int32)], axis=1)
    total_cells = ROWS * peer_count
    window_keys = jax.random.split(jax.random.fold_in(key, 105), ROWS)
    spread = jax.vmap(lambda sub_key: jax.random.permutation(sub_key, peer_count))(window_keys).astype(jnp.int32)
    seat_keys = jax.random.split(jax.random.fold_in(key, 106), peer_count)
    seat_table = jax.vmap(lambda sub_key: jax.random.permutation(sub_key, ROWS))(seat_keys).astype(jnp.int32)
    all_cells = jnp.arange(total_cells, dtype=jnp.int32)
    window = all_cells // peer_count
    member = all_cells % peer_count
    target_dev = spread[window, member]
    position = (target_dev * ROWS + seat_table[target_dev, window]).astype(jnp.int32)
    offsets = (jnp.cumsum(counts) - counts).astype(jnp.int32)
    local_idx = jnp.arange(KMAX, dtype=jnp.int32)
    is_live = local_idx[None, :] < counts[:, None]
    glob_idx = jnp.minimum(offsets[:, None] + local_idx[None, :], total_cells - 1)
    hilbert = jnp.where(is_live, position[glob_idx], -1).astype(jnp.int32)
    z_table = jnp.zeros((total_cells,), jnp.int32).at[position].set(all_cells)
    return (counts, cell_table.reshape(-1), hilbert, z_table)


def draw_row_counts(key, part):
    return layout_tables(key)[0]


def draw_cell_ids(key, part):
    return layout_tables(key)[1]


def draw_hilbert_position(key, part):
    return layout_tables(key)[2]


def draw_z_position(key, part):
    return layout_tables(key)[3]


def draw_raw_points(key, part):
    key = jax.random.fold_in(key, 7)
    total_rows = RAW_DEV * N_PTS
    row_scale = jnp.exp(jax.random.uniform(jax.random.fold_in(key, 1), (total_rows, 1), jnp.float32, jnp.log(0.3), jnp.log(3.0)))
    col_scale = jnp.exp(jax.random.uniform(jax.random.fold_in(key, 2), (1, C_IN), jnp.float32, jnp.log(0.3), jnp.log(3.0)))
    noise_val = jax.random.truncated_normal(jax.random.fold_in(key, 3), -4.0, 4.0, (total_rows, C_IN), jnp.float32)
    values = row_scale * col_scale * noise_val
    return values.astype(jnp.bfloat16)


def draw_qkv_weight(key, part):
    key = jax.random.fold_in(key, 11)
    factor = C ** (-0.5)
    first = jax.random.truncated_normal(jax.random.fold_in(key, 1), -4.0, 4.0, (C, C), jnp.float32)
    second = jax.random.truncated_normal(jax.random.fold_in(key, 2), -4.0, 4.0, (C, C), jnp.float32)
    third = jax.random.truncated_normal(jax.random.fold_in(key, 3), -4.0, 4.0, (C, C), jnp.float32)
    query_w = factor * first
    key_w = factor * second
    value_w = factor * third
    return jnp.stack([query_w, key_w, value_w]).astype(jnp.bfloat16)


def levels(stream_key, shape, shards, low, largest):
    def one(dim, shards_of):
        steps = jax.random.uniform(jax.random.fold_in(jax.random.fold_in(stream_key, 6), dim), (shards_of,), jnp.float32, low / len(shards), largest / len(shards))
        return jnp.repeat(jnp.exp(steps), shape[dim] // shards_of).reshape((-1,) + (1,) * (len(shape) - dim - 1))

    level = one(*shards[0])
    for cut in shards[1:]:
        level = level * one(*cut)
    return level


def scatter_about(rng, shape, width, reach, cuts=(), held_as=jnp.bfloat16):
    drawn = jax.random.normal(rng, shape, jnp.float32) * width
    if len(cuts) > 0:
        drawn = levels(rng, shape, cuts, -0.22, 0.18) * drawn
    return jnp.clip(drawn, min=-reach, max=reach).astype(held_as)


def setup_inputs(seed: int = 0) -> dict:
    key_list = jax.random.split(jax.random.key(seed), 11)
    return {
        "raw_points": draw_raw_points(jax.random.fold_in(key_list[10], 71), 0),
        "cell_ids": draw_cell_ids(jax.random.fold_in(key_list[10], 71), 0),
        "row_counts": draw_row_counts(jax.random.fold_in(key_list[10], 71), 0),
        "hilbert_position": draw_hilbert_position(jax.random.fold_in(key_list[10], 71), 0),
        "z_position": draw_z_position(jax.random.fold_in(key_list[10], 71), 0),
        "pool_weight": scatter_about(key_list[5], (C_IN, C), C_IN ** -0.5, 0.5),
        "qkv_weight": draw_qkv_weight(jax.random.fold_in(key_list[10], 71), 0),
        "proj_weight": scatter_about(key_list[7], (C, C), C ** -0.5, 0.375, ((1, 4),)),
        "fc1_weight": scatter_about(key_list[8], (C, FFN), C ** -0.5, 0.375, ((1, 4),)),
        "fc2_weight": scatter_about(key_list[9], (FFN, C), FFN ** -0.5, 0.1875, ((0, 4),)),
    }


eps_norm = 1e-05

def layer_norm(values):
    values = values.astype(jnp.float32)
    center = values - lax.optimization_barrier(jnp.mean(values, axis=-1, keepdims=True))
    spread = lax.optimization_barrier(jnp.mean(center * center, axis=-1, keepdims=True))
    return center * lax.rsqrt(spread + eps_norm)

def attend_patch(blocks):
    query_blk, key_blk, value_blk = blocks
    scores = jnp.einsum('hqd,hkd->hqk', query_blk.astype(jnp.float32), key_blk.astype(jnp.float32)) * HEAD_DIM ** (-0.5)
    peak = lax.optimization_barrier(jnp.max(scores, axis=-1, keepdims=True))
    raised = jnp.exp(scores - peak)
    weights = (raised / lax.optimization_barrier(jnp.sum(raised, axis=-1, keepdims=True))).astype(jnp.bfloat16)
    mixed_out = jnp.einsum('hqk,hkd->hqd', weights.astype(jnp.float32), value_blk.astype(jnp.float32))
    return mixed_out.astype(jnp.bfloat16)

def reference(raw_points, cell_ids, row_counts, hilbert_position, z_position, pool_weight, qkv_weight, proj_weight, fc1_weight, fc2_weight):
    offsets = (jnp.cumsum(row_counts) - row_counts).astype(jnp.int32)
    global_ids = (cell_ids.reshape(N_PTS, RAW_DEV) + offsets[:, None]).reshape(-1).astype(jnp.int32)
    cell_sums = jax.ops.segment_sum(raw_points.astype(jnp.float32), global_ids, num_segments=CELLS)
    cell_tally = jax.ops.segment_sum(jnp.ones(global_ids.shape, jnp.float32), global_ids, num_segments=CELLS)
    pooled = (cell_sums / cell_tally[:, None]).astype(jnp.bfloat16)
    local_idx = jnp.arange(KMAX, dtype=jnp.int32)
    is_live = local_idx[None, :] < row_counts[:, None]
    source_cell = jnp.where(is_live, offsets[:, None] + local_idx[None, :], 0).reshape(-1).astype(jnp.int32)
    target_row = jnp.where(is_live, hilbert_position, CELLS).reshape(-1).astype(jnp.int32)
    in_order = jnp.zeros((CELLS + 1, C_IN), jnp.bfloat16).at[target_row].set(pooled[source_cell])[:CELLS]
    features = jnp.dot(in_order, pool_weight, preferred_element_type=jnp.float32).astype(jnp.bfloat16)
    normed = layer_norm(features).astype(jnp.bfloat16)
    query = jnp.dot(normed, qkv_weight[0], preferred_element_type=jnp.float32).astype(jnp.bfloat16)
    keys = jnp.dot(normed, qkv_weight[1], preferred_element_type=jnp.float32).astype(jnp.bfloat16)
    values = jnp.dot(normed, qkv_weight[2], preferred_element_type=jnp.float32).astype(jnp.bfloat16)
    patch_count = CELLS // PATCH

    def split_heads(matrix):
        return matrix.reshape(patch_count, PATCH, HEADS, HEAD_DIM).transpose(0, 2, 1, 3)
    attended = lax.map(attend_patch, (split_heads(query), split_heads(keys), split_heads(values)))
    attended = attended.transpose(0, 2, 1, 3).reshape(CELLS, C)
    mixture = jnp.dot(attended, proj_weight, preferred_element_type=jnp.float32)
    block_mid = (features.astype(jnp.float32) + mixture).astype(jnp.bfloat16)
    normed2 = layer_norm(block_mid).astype(jnp.bfloat16)
    hidden = jax.nn.gelu(jnp.dot(normed2, fc1_weight, preferred_element_type=jnp.float32), approximate=False).astype(jnp.bfloat16)
    result = (block_mid.astype(jnp.float32) + jnp.dot(hidden, fc2_weight, preferred_element_type=jnp.float32)).astype(jnp.bfloat16)
    return jnp.zeros((CELLS, C), jnp.bfloat16).at[z_position].set(result)
```

```python
import jax
import jax.numpy as jnp
from jax import lax
from jax.experimental import pallas as pl
from jax.experimental.pallas import tpu as pltpu
from jax.sharding import PartitionSpec as P

BF16 = jnp.bfloat16
EPS = 1e-5
MESH = pl.DeviceIdType.MESH
NZ = 16


def place():
    p, c = lax.axis_index("pts"), lax.axis_index("ch")
    return p // 32, lax.rem(p // 2, NZ), lax.rem(p, 2), c


def dev(y, z, k, c):
    return (y * 32 + z * 2 + k, c)


def gather_kernel(slots, pos, pack, rows, posz, wall, mid, s1, r1, s2, r2, s3, r3, ps, pr, ws, wr, fs, fr, loc):
    y, z, k, c = place()
    barrier = pltpu.get_barrier_semaphore()
    off_diag = y != c

    def hello(d):
        pl.semaphore_signal(barrier, inc=1, device_id=d, device_id_type=MESH)

    hello(dev(c, z, 1 - k, y))

    @pl.when(off_diag)
    def _():
        hello(dev(c, z, k, y))
    hello(dev(y, z, 1 - k, c))
    for i in range(1, 4):
        hello(dev(y, z, k, lax.rem(c + i, 4)))

    @pl.loop(1, NZ)
    def _(i):
        hello(dev(y, lax.rem(z + i, NZ), k, c))

    @pl.when(off_diag)
    def _():
        pl.semaphore_wait(barrier, 21)

    @pl.when(jnp.logical_not(off_diag))
    def _():
        pl.semaphore_wait(barrier, 20)

    def stage1(kk):
        return pltpu.make_async_remote_copy(
            src_ref=slots.at[kk], dst_ref=mid.at[:, k], send_sem=s1.at[kk], recv_sem=r1.at[k],
            device_id=dev(c, z, kk, y), device_id_type=MESH)

    def stage1_own():
        return pltpu.make_async_copy(slots.at[k], mid.at[:, k], r1.at[k])

    other = stage1(1 - k)
    other.start()

    @pl.when(off_diag)
    def _():
        stage1(k).start()

    @pl.when(jnp.logical_not(off_diag))
    def _():
        stage1_own().start()

    def pos1(i):
        zz = lax.rem(z + i, NZ)
        return pltpu.make_async_remote_copy(
            src_ref=pos.at[zz], dst_ref=posz.at[z], send_sem=ps.at[i], recv_sem=pr.at[i],
            device_id=dev(y, zz, k, c), device_id_type=MESH)

    own_pos = pltpu.make_async_copy(pos.at[z], posz.at[z], loc.at[0])
    own_pos.start()

    @pl.loop(1, NZ)
    def _(i):
        pos1(i).start()

    HALF = pack.shape[0] // 2
    half = pl.ds(pl.multiple_of(k * HALF, HALF), HALF)
    own_w = pltpu.make_async_copy(pack, wall.at[c], loc.at[1])
    own_w.start()

    def wx(i):
        return pltpu.make_async_remote_copy(
            src_ref=pack.at[half], dst_ref=wall.at[c, half], send_sem=ws.at[i], recv_sem=wr.at[i],
            device_id=dev(y, z, k, lax.rem(c + i, 4)), device_id_type=MESH)
    for i in range(1, 4):
        wx(i).start()

    def mine(kk):
        return pltpu.make_async_copy(slots.at[kk], mid.at[:, kk], r1.at[kk])
    mine(0).wait()
    mine(1).wait()

    def stage2(i):
        zz = lax.rem(z + i, NZ)
        return pltpu.make_async_remote_copy(
            src_ref=mid.at[zz], dst_ref=rows.at[c, z], send_sem=s2.at[i], recv_sem=r2.at[i],
            device_id=dev(y, zz, k, c), device_id_type=MESH)

    @pl.loop(1, NZ)
    def _(i):
        stage2(i).start()
    own = pltpu.make_async_copy(mid.at[z], rows.at[c, z], loc.at[2])
    own.start()
    own.wait()

    def stage3(i, j):
        zs = lax.rem(z - i + NZ, NZ)
        return pltpu.make_async_remote_copy(
            src_ref=rows.at[c, zs], dst_ref=rows.at[c, zs], send_sem=s3.at[i, j], recv_sem=r3.at[i, j],
            device_id=dev(y, z, k, lax.rem(c + j, 4)), device_id_type=MESH)
    for j in range(1, 4):
        stage3(0, j).start()

    @pl.loop(1, NZ)
    def _(i):
        stage2(i).wait_recv()
        for j in range(1, 4):
            stage3(i, j).start()

    own_pos.wait()


    def wf(i):
        src = lax.rem(c - i + 4, 4)
        return pltpu.make_async_remote_copy(
            src_ref=wall.at[src, half], dst_ref=wall.at[src, half], send_sem=fs.at[i], recv_sem=fr.at[i],
            device_id=dev(y, z, 1 - k, c), device_id_type=MESH)
    for i in range(1, 4):
        wx(i).wait_recv()
        wf(i).start()

    own_w.wait()

    @pl.loop(1, NZ)
    def _(i):
        pos1(i).wait()
        stage2(i).wait_send()

    @pl.loop(0, NZ)
    def _(i):
        for j in range(1, 4):
            stage3(i, j).wait()
    for i in range(1, 4):
        wx(i).wait_send()
        wf(i).wait()
    other.wait_send()

    @pl.when(off_diag)
    def _():
        stage1(k).wait_send()


def regroup(slots, pos, pack):
    DMA = pltpu.SemaphoreType.DMA
    any_ = pl.BlockSpec(memory_space=pl.ANY)
    vm = pl.BlockSpec(memory_space=pltpu.VMEM)
    return pl.pallas_call(
        gather_kernel,
        out_shape=(
            jax.ShapeDtypeStruct((4, NZ, 2, 16, 128), jnp.bfloat16),
            jax.ShapeDtypeStruct((NZ, 1, 128), jnp.int32),
            jax.ShapeDtypeStruct((4,) + pack.shape, jnp.bfloat16),
        ),
        in_specs=[vm, vm, any_],
        out_specs=(vm, vm, any_),
        scratch_shapes=[
            pltpu.VMEM((NZ, 2, 16, 128), jnp.bfloat16),
            DMA((2,)), DMA((2,)), DMA((NZ,)), DMA((NZ,)), DMA((NZ, 4)), DMA((NZ, 4)),
            DMA((NZ,)), DMA((NZ,)), DMA((4,)), DMA((4,)), DMA((4,)), DMA((4,)), DMA((3,)),
        ],
        compiler_params=pltpu.CompilerParams(collective_id=0, has_side_effects=True,
                                             vmem_limit_bytes=32 * 1024 * 1024),
        name="regroup_rows",
    )(slots, pos, pack)


def return_kernel(out, posz, back, posall, mid, s1, r1, ps, pr, s2, r2, loc):
    y, z, k, c = place()
    barrier = pltpu.get_barrier_semaphore()
    on_diag = y == c
    me = y * 2 + k

    def hello(d):
        pl.semaphore_signal(barrier, inc=1, device_id=d, device_id_type=MESH)

    @pl.loop(0, 8)
    def _(i):
        ys, ks = i // 2, lax.rem(i, 2)

        @pl.when(jnp.logical_not(on_diag & (i == me)))
        def _():
            hello(dev(ys, z, ks, y))

    @pl.loop(1, NZ)
    def _(i):
        hello(dev(y, lax.rem(z + i, NZ), k, c))

    @pl.when(on_diag)
    def _():
        pl.semaphore_wait(barrier, 22)

    @pl.when(jnp.logical_not(on_diag))
    def _():
        pl.semaphore_wait(barrier, 23)

    def stage1(i):
        kk, cc = lax.rem(i, 2), i // 2
        d = dev(c, z, kk, cc)
        a = pltpu.make_async_remote_copy(
            src_ref=out.at[kk, cc], dst_ref=mid.at[me], send_sem=s1.at[i], recv_sem=r1.at[me],
            device_id=d, device_id_type=MESH)
        b = pltpu.make_async_remote_copy(
            src_ref=posz, dst_ref=posall.at[me], send_sem=ps.at[i], recv_sem=pr.at[me],
            device_id=d, device_id_type=MESH)
        return a, b

    def is_me(i):
        return on_diag & (i == c * 2 + k)

    @pl.loop(0, 8)
    def _(i):
        @pl.when(is_me(i))
        def _():
            pltpu.make_async_copy(out.at[k, c], mid.at[me], r1.at[me]).start()
            pltpu.make_async_copy(posz, posall.at[me], pr.at[me]).start()

        @pl.when(jnp.logical_not(is_me(i)))
        def _():
            a, b = stage1(i)
            a.start()
            b.start()

    def arrived(i):
        return (pltpu.make_async_copy(mid.at[i], mid.at[i], r1.at[i]),
                pltpu.make_async_copy(posall.at[i], posall.at[i], pr.at[i]))

    @pl.loop(0, 8)
    def _(i):
        arrived(i)[0].wait()

    def stage2(i):
        zz = lax.rem(z + i, NZ)
        return pltpu.make_async_remote_copy(
            src_ref=mid.at[:, zz], dst_ref=back.at[z], send_sem=s2.at[i], recv_sem=r2.at[i],
            device_id=dev(y, zz, k, c), device_id_type=MESH)

    @pl.loop(1, NZ)
    def _(i):
        stage2(i).start()
    own = pltpu.make_async_copy(mid.at[:, z], back.at[z], loc.at[0])
    own.start()
    own.wait()

    @pl.loop(0, 8)
    def _(i):
        arrived(i)[1].wait()

        @pl.when(jnp.logical_not(is_me(i)))
        def _():
            a, b = stage1(i)
            a.wait_send()
            b.wait_send()

    @pl.loop(1, NZ)
    def _(i):
        stage2(i).wait()


def send_back(out, posz):
    DMA = pltpu.SemaphoreType.DMA
    vm = pl.BlockSpec(memory_space=pltpu.VMEM)
    return pl.pallas_call(
        return_kernel,
        out_shape=(
            jax.ShapeDtypeStruct((NZ, 8, 4, 128), jnp.bfloat16),
            jax.ShapeDtypeStruct((8, NZ, 1, 128), jnp.int32),
        ),
        in_specs=[vm, vm],
        out_specs=(vm, vm),
        scratch_shapes=[
            pltpu.VMEM((8, NZ, 4, 128), jnp.bfloat16),
            DMA((8,)), DMA((8,)), DMA((8,)), DMA((8,)), DMA((NZ,)), DMA((NZ,)), DMA((1,)),
        ],
        compiler_params=pltpu.CompilerParams(collective_id=1, has_side_effects=True,
                                             vmem_limit_bytes=32 * 1024 * 1024),
        name="return_rows",
    )(out, posz)
def iota(shape, dim):
    return lax.broadcasted_iota(jnp.int32, shape, dim)


def dot(a, b):
    return jnp.dot(a, b, preferred_element_type=jnp.float32)


def dot_nt(a, b):
    return lax.dot_general(a, b, (((1,), (1,)), ((), ())), preferred_element_type=jnp.float32)


def onehot(mask):
    return jnp.where(mask, 1.0, 0.0).astype(BF16)


def row_norm(values):
    center = values - jnp.mean(values, axis=-1, keepdims=True)
    spread = jnp.mean(center * center, axis=-1, keepdims=True)
    return (center * lax.rsqrt(spread + EPS)).astype(BF16)


def column_norm(values):
    center = values - jnp.mean(values, axis=0, keepdims=True)
    spread = jnp.mean(center * center, axis=0, keepdims=True)
    return (center * lax.rsqrt(spread + EPS)).astype(BF16)


def pool_kernel(raw, ids, hilbert, zpos, qkv, proj, fc1, fc2, slots, pos, pack):
    c = lax.axis_index("ch")
    target = hilbert[...]
    rel = jnp.where(target >= 0, (target >> 10) - c * 32, -1)
    hits = iota((32, 2048), 0) == rel
    hot = onehot(hits)
    upper = onehot(iota((256, 256), 0) < iota((256, 256), 1))
    before = jnp.zeros((32, 1), jnp.float32)
    index_rows = []
    for b in range(8):
        part = hot[:, b * 256:(b + 1) * 256]
        part32 = part.astype(jnp.float32)
        rank = dot(part, upper) + before
        rank = jnp.sum(rank * part32, axis=0, keepdims=True)
        before = before + jnp.sum(part32, axis=1, keepdims=True)
        r = rel[:, b * 256:(b + 1) * 256]
        slot = (r & 1) * 256 + (r >> 1) * 16 + rank.astype(jnp.int32)
        index_rows.append(jnp.where((r >= 0) & (r < 32), slot, -1))
    cell = jnp.zeros((512, 256), jnp.float32)
    for b in range(8):
        place_ = onehot(iota((512, 256), 0) == index_rows[b])
        low = iota((256, 256), 1) >= 128
        number = jnp.where(low, iota((256, 256), 0), b).astype(jnp.float32).astype(BF16)
        cell = cell + dot(place_, number)
    cell = cell[:, :128] * 256.0 + cell[:, 128:]
    total = jnp.zeros((512, 256), jnp.float32)
    one = jnp.ones((512, 128), BF16)
    points = ids[...].astype(jnp.float32)
    for b in range(6):
        member = jnp.concatenate(
            [onehot(cell == points[4 * b + j:4 * b + j + 1]) for j in range(4)], axis=1)
        rows = jnp.concatenate([raw[b * 512:(b + 1) * 512], one], axis=1)
        total = total + dot(member, rows)
    mean = (total[:, :128] / total[:, 128:]).astype(BF16)
    for kk in range(2):
        for zz in range(16):
            at = kk * 256 + zz * 16
            slots[kk, zz] = mean[at:at + 16]
    z_rows = zpos[...]
    z32 = z_rows.astype(jnp.float32)
    column = jnp.concatenate(
        [jnp.transpose(jnp.broadcast_to(z32[j:j + 1], (128, 128))) for j in range(8)], axis=0)
    split = jnp.zeros((32, 128), jnp.float32)
    for j in range(8):
        rank = jnp.sum(jnp.where(column < z32[j:j + 1], 1.0, 0.0), axis=0, keepdims=True)
        rank = rank.astype(jnp.int32)
        own = z_rows[j:j + 1] & 1023
        dest = rank >> 3
        z_of = (dest >> 1) & 15
        lane = ((dest >> 5) * 2 + (dest & 1)) * 8 + (rank & 7)
        sub = iota((32, 128), 0)
        digit = jnp.where(sub < 16, own >> 5, own & 31).astype(jnp.float32)
        left = jnp.where((sub & 15) == z_of, digit, 0.0).astype(BF16)
        right = onehot(iota((128, 128), 0) == lane)
        split = split + dot_nt(left, right)
    table = (split[:16] * 32.0 + split[16:]).astype(jnp.int32)
    for zz in range(16):
        pos[zz] = table[zz:zz + 1]
    eye = onehot(iota((256, 256), 0) == iota((256, 256), 1))
    eye64 = onehot(iota((64, 64), 0) == iota((64, 64), 1))
    for t in range(3):
        pack[t * 64:(t + 1) * 64] = dot_nt(eye64, qkv[t]).astype(BF16)
    pack[192:256] = dot_nt(eye64, proj[...]).astype(BF16)
    pack[256:512] = dot_nt(eye, fc1[...]).astype(BF16)
    pack[512:768] = dot_nt(eye, fc2[...]).astype(BF16)


def block_kernel(rows, counts, pool, wall, out, x_ref):
    c = lax.axis_index("ch")
    f32 = jnp.float32
    units = (counts[...] >> 7).astype(f32).astype(BF16)
    units = jnp.broadcast_to(units, (8, 128))
    source = iota((128, 2048), 1) >> 4
    held = dot(units, onehot(iota((128, 2048), 0) == source))[:1].astype(jnp.int32)
    first = dot(units, onehot(iota((128, 2048), 0) < source))[:1].astype(jnp.int32)
    within = iota((1, 2048), 1) & 15
    order = jnp.where(within < held, first + within, -1)
    x = jnp.zeros((1024, 128), f32)
    for b in range(8):
        sel = onehot(iota((1024, 256), 0) == order[:, b * 256:(b + 1) * 256])
        x = x + dot(sel, rows[b * 256:(b + 1) * 256])
    x = x.astype(BF16)
    x_ref[...] = x
    w = pool[...]
    normed = row_norm(dot(x, w).astype(BF16).astype(f32))
    wq = jnp.concatenate([wall[i, 0:64] for i in range(4)], axis=0)
    wk = jnp.concatenate([wall[i, 64:128] for i in range(4)], axis=0)
    wv = jnp.concatenate([wall[i, 128:192] for i in range(4)], axis=0)
    keys = dot_nt(normed, wk).astype(BF16)
    values = dot_nt(wv, normed).astype(BF16)
    t = iota((256, 256), 0)
    row = 8 * (((t >> 2) & 15) * 2 + ((t >> 6) & 1)) + 4 * (t >> 7) + (t & 3)
    mine = dot(onehot(iota((256, 256), 1) == row), x_ref[pl.ds(pl.multiple_of(c * 256, 256), 256)])
    features = dot(mine.astype(BF16), w).astype(BF16).astype(f32)
    query = dot_nt(wq, row_norm(features)).astype(BF16)
    head_of = iota((256, 256), 0) >> 4
    ones = jnp.ones((16, 1024), BF16)
    scale = 0.25 * 1.4426950408889634
    heads = []
    for h in range(16):
        only = jnp.where(head_of == h, query.astype(f32), 0.0).astype(BF16)
        scores = dot(keys, only)
        peak = jnp.max(scores, axis=0, keepdims=True)
        raised = jnp.exp2((scores - peak) * scale).astype(BF16)
        mix = dot(jnp.concatenate([values[h * 16:(h + 1) * 16], ones], axis=0), raised)
        heads.append((mix[:16] / mix[16:17]).astype(BF16))
    attended = jnp.concatenate(heads, axis=0)
    wp = jnp.concatenate([wall[i, 192:256] for i in range(4)], axis=0)
    middle = (jnp.transpose(features) + dot(wp, attended)).astype(BF16).astype(f32)
    normed2 = column_norm(middle)
    total = jnp.zeros((256, 256), f32)
    for i in range(4):
        v = dot(wall[i, 256:512], normed2)
        hidden = (v * (1.0 + lax.erf(v * 0.7071067811865476)) * 0.5).astype(BF16)
        total = total + dot(wall[i, 512:768], hidden)
    result = jnp.transpose(middle + total)
    for kk in range(2):
        for cc in range(4):
            both = [result[h * 128 + kk * 64:h * 128 + kk * 64 + 64, cc * 64:cc * 64 + 64] for h in range(2)]
            out[kk, cc] = jnp.concatenate(both, axis=1).reshape(16, 4, 128).astype(BF16)


def settle_kernel(back, posall, out):
    p = lax.axis_index("pts")
    me = (p // 32) * 2 + lax.rem(p, 2)
    f32 = jnp.float32
    got = back[...].astype(f32).reshape(512, 128).astype(BF16)
    table = posall[...].reshape(128, 128)
    pick = onehot(iota((8, 128), 1) == me * 8 + iota((8, 128), 0))
    digits = [dot_nt(pick, part.astype(f32).astype(BF16)).astype(BF16) for part in (table >> 5, table & 31)]
    k = iota((128, 512), 1)
    spread = onehot(iota((128, 512), 0) == ((k >> 2) & 7) * 16 + (k >> 5))
    full = dot(digits[0], spread) * 32.0 + dot(digits[1], spread)
    sub, lane = iota((8, 512), 0), iota((8, 512), 1)
    halves = []
    for h in range(2):
        want = jnp.sum(jnp.where(sub == h * 4 + (lane & 3), full, 0.0), axis=0, keepdims=True)
        want = want.astype(jnp.int32)
        halves.append(dot(onehot(iota((1024, 512), 0) == want), got))
    out[...] = (halves[0][:, :64] + halves[1][:, 64:]).astype(BF16)


def local(body, out_shape, scratch=(), name=None):
    n_out = len(out_shape) if isinstance(out_shape, tuple) else 1
    vm = pl.BlockSpec(memory_space=pltpu.VMEM)
    return pl.pallas_call(
        body, out_shape=out_shape,
        out_specs=(vm,) * n_out if isinstance(out_shape, tuple) else vm,
        scratch_shapes=scratch,
        compiler_params=pltpu.CompilerParams(vmem_limit_bytes=48 * 1024 * 1024), name=name)


def shards(raw_points, cell_ids, row_counts, hilbert_position, z_position,
           pool_weight, qkv_weight, proj_weight, fc1_weight, fc2_weight):
    S = jax.ShapeDtypeStruct
    slots, pos, pack = local(
        pool_kernel,
        (S((2, NZ, 16, 128), BF16), S((NZ, 1, 128), jnp.int32), S((768, 256), BF16)),
        name="pool_cells",
    )(raw_points, cell_ids.reshape(24, 128), hilbert_position, z_position.reshape(8, 128),
      qkv_weight, proj_weight, fc1_weight, fc2_weight)
    rows, posz, wall = regroup(slots, pos, pack)
    out = local(
        block_kernel, S((2, 4, NZ, 4, 128), BF16), scratch=[pltpu.VMEM((1024, 128), BF16)],
        name="block",
    )(rows.reshape(2048, 128), row_counts.reshape(1, 128), pool_weight, wall)
    back, posall = send_back(out, posz)
    return local(settle_kernel, S((1024, 64), BF16), name="settle")(back, posall)


def solution(mesh):
    in_specs = (P("pts", None), P("pts"), P(), P("pts", None), P("pts"), P(),
                P(None, None, "ch"), P(None, "ch"), P(None, "ch"), P("ch", None))
    return jax.shard_map(shards, mesh=mesh, in_specs=in_specs, out_specs=P("pts", "ch"),
                         check_vma=False)
```

```python
import jax
import jax.numpy as jnp
from jax import lax
from jax.experimental import pallas as pl
from jax.experimental.pallas import tpu as pltpu
from jax.sharding import PartitionSpec as P

BF16 = jnp.bfloat16
EPS = 1e-5


def iota(shape, dim):
    return lax.broadcasted_iota(jnp.int32, shape, dim)


def dot(a, b):
    return jnp.dot(a, b, preferred_element_type=jnp.float32)


def dot_nt(a, b):
    return lax.dot_general(a, b, (((1,), (1,)), ((), ())), preferred_element_type=jnp.float32)


def onehot(mask):
    return jnp.where(mask, 1.0, 0.0).astype(BF16)


def row_norm(values):
    center = values - jnp.mean(values, axis=-1, keepdims=True)
    spread = jnp.mean(center * center, axis=-1, keepdims=True)
    return (center * lax.rsqrt(spread + EPS)).astype(BF16)


MESH = pl.DeviceIdType.MESH
NZ = 16
LIMIT = 64 * 1024 * 1024 - 65536
ANY = pl.BlockSpec(memory_space=pltpu.HBM)
VM = pl.BlockSpec(memory_space=pltpu.VMEM)


def place():
    p, c = lax.axis_index("pts"), lax.axis_index("ch")
    return p // 32, lax.rem(p // 2, NZ), lax.rem(p, 2), c


def dev(y, z, k, c):
    return (y * 32 + z * 2 + k, c)


def hop(j):
    return lax.rem(j, 2) * ((j + 1) // 2) + (1 - lax.rem(j, 2)) * (NZ - j // 2)


def layer_kernel(raw_h, ids_h, hilbert_h, zpos_h, counts_h, pool_h, qkv_h, proj_h, fc1_h, fc2_h,
                 result_t,
                 raw, ids, hilbert, zpos, counts, pool, wq, wp, w1, w2,
                 slots, pos, posz, posall, mid, rows, acc, out, mid2,
                 lsem, ps, pr, s2, r2, s3, r3, ws, wr, fs, fr, qs, qr, c1s, c1r, c2s, c2r, back, placing):
    y, z, k, c = place()
    me = y * 2 + k
    f32 = jnp.float32
    on_diag = y == c
    barrier = pltpu.get_barrier_semaphore()

    def hello(d):
        pl.semaphore_signal(barrier, inc=1, device_id=d, device_id_type=MESH)

    hello(dev(y, z, 1 - k, c))
    for i in range(1, 4):
        hello(dev(y, z, k, lax.rem(c + i, 4)))

    @pl.loop(1, NZ)
    def _(i):
        hello(dev(y, lax.rem(z + i, NZ), k, c))

    @pl.loop(0, 8)
    def _(i):
        @pl.when(jnp.logical_not(on_diag & (i == me)))
        def _():
            hello(dev(i // 2, z, lax.rem(i, 2), y))

    loads = [pltpu.make_async_copy(a, b, lsem.at[i]) for i, (a, b) in enumerate((
        (hilbert_h, hilbert), (zpos_h, zpos), (ids_h, ids), (raw_h, raw), (counts_h, counts), (pool_h, pool),
        (qkv_h, wq.at[c]), (proj_h, wp.at[c]), (fc1_h, w1.at[c]), (fc2_h, w2.at[c])))]
    for load in loads:
        load.start()

    loads[0].wait()
    target = hilbert[...]
    rel = jnp.where(target >= 0, (target >> 10) - c * 32, -1)
    hot = onehot(iota((32, 2048), 0) == rel)
    upper = onehot(iota((256, 256), 0) < iota((256, 256), 1))
    before = jnp.zeros((32, 1), f32)
    cell = jnp.zeros((512, 256), f32)
    for b in range(8):
        part = hot[:, b * 256:(b + 1) * 256]
        part32 = part.astype(f32)
        rank = jnp.sum((dot(part, upper) + before) * part32, axis=0, keepdims=True)
        before = before + jnp.sum(part32, axis=1, keepdims=True)
        r = rel[:, b * 256:(b + 1) * 256]
        index = jnp.where((r >= 0) & (r < 32), r * 16 + rank.astype(jnp.int32), -1)
        number = jnp.where(iota((256, 256), 1) >= 128, iota((256, 256), 0), b)
        cell = cell + dot(onehot(iota((512, 256), 0) == index), number.astype(f32).astype(BF16))
    cell = cell[:, :128] * 256.0 + cell[:, 128:]

    @pl.when(on_diag)
    def _():
        pl.semaphore_wait(barrier, 26)

    @pl.when(jnp.logical_not(on_diag))
    def _():
        pl.semaphore_wait(barrier, 27)

    def parts(a):
        return ((qkv_h, wq, 32, True), (fc1_h, w1, 128, False), (proj_h, wp, 32, False),
                (fc2_h, w2, 128, False))[a]

    def weight_x(a, i):
        src, dst, size, deep = parts(a)
        half = pl.ds(pl.multiple_of(k * size, size), size)
        return pltpu.make_async_remote_copy(
            src_ref=src.at[:, half] if deep else src.at[half],
            dst_ref=dst.at[c, :, half] if deep else dst.at[c, half],
            send_sem=ws.at[a, i], recv_sem=wr.at[a, i],
            device_id=dev(y, z, k, lax.rem(c + i, 4)), device_id_type=MESH)

    def weight_core(a, i):
        _, dst, size, deep = parts(a)
        half = pl.ds(pl.multiple_of(k * size, size), size)
        owner = lax.rem(c - i + 4, 4)
        at = dst.at[owner, :, half] if deep else dst.at[owner, half]
        return pltpu.make_async_remote_copy(
            src_ref=at, dst_ref=at, send_sem=fs.at[a, i], recv_sem=fr.at[a, i],
            device_id=dev(y, z, 1 - k, c), device_id_type=MESH)

    for a in range(4):
        for i in range(1, 4):
            weight_x(a, i).start()

    loads[2].wait()
    loads[3].wait()
    total = jnp.zeros((512, 256), f32)
    one = jnp.ones((512, 128), BF16)
    points = ids[...].astype(f32)
    for b in range(6):
        member = jnp.concatenate(
            [onehot(cell == points[4 * b + j:4 * b + j + 1]) for j in range(4)], axis=1)
        total = total + dot(member, jnp.concatenate([raw[b * 512:(b + 1) * 512], one], axis=1))
    mean = (total[:, :128] / total[:, 128:]).astype(BF16)
    for zz in range(NZ):
        for kk in range(2):
            slots[zz, kk] = mean[zz * 32 + kk * 16:zz * 32 + kk * 16 + 16]

    def rows_z(j):
        zz = lax.rem(z + hop(j), NZ)
        return pltpu.make_async_remote_copy(
            src_ref=slots.at[zz], dst_ref=mid.at[j], send_sem=s2.at[j], recv_sem=r2.at[j],
            device_id=dev(y, zz, k, c), device_id_type=MESH)

    @pl.loop(1, NZ)
    def _(j):
        rows_z(j).start()
    own_z = pltpu.make_async_copy(slots.at[z], mid.at[0], r2.at[0])
    own_z.start()

    def is_me(i):
        return on_diag & (i == c * 2 + k)

    def on(g, i):
        kk, cc = lax.rem(i, 2), i // 2
        return pltpu.make_async_remote_copy(
            src_ref=mid.at[2 * g:2 * g + 2, kk], dst_ref=rows.at[2 * g:2 * g + 2, me],
            send_sem=s3.at[g, i], recv_sem=r3.at[g, me],
            device_id=dev(c, z, kk, cc), device_id_type=MESH)

    def on_start(g):
        @pl.loop(0, 8)
        def _(i):
            @pl.when(is_me(i))
            def _():
                pltpu.make_async_copy(mid.at[2 * g:2 * g + 2, k], rows.at[2 * g:2 * g + 2, me],
                                      r3.at[g, me]).start()

            @pl.when(jnp.logical_not(is_me(i)))
            def _():
                on(g, i).start()

    def on_arrived(g):
        @pl.loop(0, 8)
        def _(i):
            block = rows.at[2 * g:2 * g + 2, i]
            pltpu.make_async_copy(block, block, r3.at[g, i]).wait()

    loads[1].wait()
    z_rows = zpos[...]
    z32 = z_rows.astype(f32)
    column = jnp.concatenate(
        [jnp.transpose(jnp.broadcast_to(z32[j:j + 1], (128, 128))) for j in range(8)], axis=0)
    split = jnp.zeros((32, 128), f32)
    for j in range(8):
        rank = jnp.sum(jnp.where(column < z32[j:j + 1], 1.0, 0.0), axis=0, keepdims=True)
        rank = rank.astype(jnp.int32)
        own = z_rows[j:j + 1] & 1023
        dest = rank >> 3
        lane = ((dest >> 5) * 2 + (dest & 1)) * 8 + (rank & 7)
        sub = iota((32, 128), 0)
        digit = jnp.where(sub < 16, own >> 5, own & 31).astype(f32)
        left = jnp.where((sub & 15) == ((dest >> 1) & 15), digit, 0.0).astype(BF16)
        split = split + dot_nt(left, onehot(iota((128, 128), 0) == lane))
    table = (split[:16] * 32.0 + split[16:]).astype(jnp.int32)
    for zz in range(NZ):
        pos[zz] = table[zz:zz + 1]

    def pos_z(j):
        zz = lax.rem(z + j, NZ)
        return pltpu.make_async_remote_copy(
            src_ref=pos.at[zz], dst_ref=posz.at[z], send_sem=ps.at[j], recv_sem=pr.at[j],
            device_id=dev(y, zz, k, c), device_id_type=MESH)

    def pos_arrived(j):
        zs = lax.rem(z - j + NZ, NZ)
        return pltpu.make_async_copy(posz.at[zs], posz.at[zs], pr.at[j])

    own_pos = pltpu.make_async_copy(pos.at[z], posz.at[z], pr.at[0])
    own_pos.start()

    loads[4].wait()
    units = jnp.broadcast_to((counts[...] >> 7).astype(f32).astype(BF16), (8, 128))
    col = iota((128, 2048), 1)
    hop_no, from_yc = col >> 7, (col >> 4) & 7
    away = jnp.where((hop_no & 1) == 1, (hop_no + 1) >> 1, NZ - (hop_no >> 1))
    source = (from_yc >> 1) * 32 + ((z + NZ - away) & 15) * 2 + (from_yc & 1)
    held = dot(units, onehot(iota((128, 2048), 0) == source))[:1].astype(jnp.int32)
    first = dot(units, onehot(iota((128, 2048), 0) < source))[:1].astype(jnp.int32)
    within = iota((1, 2048), 1) & 15
    order = jnp.where(within < held, first + within, -1)

    def gather_group(g):
        on_arrived(g)
        sel = onehot(iota((1024, 256), 0) == order[:, g * 256:(g + 1) * 256])
        piece = dot(sel, rows[2 * g:2 * g + 2].reshape(256, 128))
        if g == 0:
            acc[...] = piece
        else:
            acc[...] += piece

    LAG = 3
    for g in range(8):
        for j in (2 * g, 2 * g + 1):
            pltpu.make_async_copy(mid.at[j], mid.at[j], r2.at[j]).wait()
        on_start(g)
        if g == 0:
            @pl.loop(1, NZ)
            def _(j):
                pos_z(j).start()
        if g >= LAG:
            gather_group(g - LAG)
    for a in range(4):
        for i in range(1, 4):
            weight_x(a, i).wait_recv()
            weight_core(a, i).start()
        if a == 0:
            for g in range(8 - LAG, 8):
                gather_group(g)

    @pl.loop(0, NZ)
    def _(j):
        pos_arrived(j).wait()

    def pos_on(i):
        return pltpu.make_async_remote_copy(
            src_ref=posz, dst_ref=posall.at[me], send_sem=qs.at[i], recv_sem=qr.at[me],
            device_id=dev(c, z, lax.rem(i, 2), i // 2), device_id_type=MESH)

    @pl.loop(0, 8)
    def _(i):
        @pl.when(is_me(i))
        def _():
            pltpu.make_async_copy(posz, posall.at[me], qr.at[me]).start()

        @pl.when(jnp.logical_not(is_me(i)))
        def _():
            pos_on(i).start()

    x = acc[...].astype(BF16)
    loads[5].wait()
    w = pool[...]
    normed = row_norm(dot(x, w).astype(BF16).astype(f32))
    t = iota((256, 256), 0)
    row = 8 * (((t >> 2) & 15) * 2 + ((t >> 6) & 1)) + 4 * (t >> 7) + (t & 3)
    quarter = acc[pl.ds(pl.multiple_of(c * 256, 256), 256)].astype(BF16)
    mine = dot(onehot(iota((256, 256), 1) == row), quarter)
    features = dot(mine.astype(BF16), w).astype(BF16).astype(f32)
    loads[6].wait()
    for i in range(1, 4):
        weight_core(0, i).wait_recv()
    keys = dot_nt(normed, wq[:, 1].reshape(256, 256)).astype(BF16)
    values = dot_nt(wq[:, 2].reshape(256, 256), normed).astype(BF16)
    query = dot_nt(wq[:, 0].reshape(256, 256), row_norm(features)).astype(BF16)
    head_of = iota((256, 256), 0) >> 4
    ones = jnp.ones((16, 1024), BF16)
    scale = 0.25 * 1.4426950408889634
    heads = []
    for h in range(16):
        only = jnp.where(head_of == h, query.astype(f32), 0.0).astype(BF16)
        scores = dot(keys, only)
        peak = jnp.max(scores, axis=0, keepdims=True)
        raised = jnp.exp2((scores - peak) * scale).astype(BF16)
        mix = dot(jnp.concatenate([values[h * 16:(h + 1) * 16], ones], axis=0), raised)
        heads.append((mix[:16] / mix[16:17]).astype(BF16))
    attended = jnp.concatenate(heads, axis=0)
    for load in loads[7:]:
        load.wait()
    for a in range(1, 4):
        for i in range(1, 4):
            weight_core(a, i).wait_recv()
    mixture = jnp.transpose(dot(wp[...].reshape(256, 256), attended))
    middle = (features + mixture).astype(BF16).astype(f32)
    normed2 = row_norm(middle)
    result = middle
    for i in range(4):
        v = dot(normed2, w1[i])
        hidden = (v * (1.0 + lax.erf(v * 0.7071067811865476)) * 0.5).astype(BF16)
        result = result + dot(hidden, w2[i])
    for kk in range(2):
        for cc in range(4):
            both = [result[h * 128 + kk * 64:h * 128 + kk * 64 + 64, cc * 64:cc * 64 + 64] for h in range(2)]
            out[kk, cc] = jnp.concatenate(both, axis=1).reshape(NZ, 4, 128).astype(BF16)

    def back_xy(i):
        kk, cc = lax.rem(i, 2), i // 2
        return pltpu.make_async_remote_copy(
            src_ref=out.at[kk, cc], dst_ref=mid2.at[me], send_sem=c1s.at[i], recv_sem=c1r.at[me],
            device_id=dev(c, z, kk, cc), device_id_type=MESH)

    @pl.loop(0, 8)
    def _(i):
        @pl.when(is_me(i))
        def _():
            pltpu.make_async_copy(out.at[k, c], mid2.at[me], c1r.at[me]).start()

        @pl.when(jnp.logical_not(is_me(i)))
        def _():
            back_xy(i).start()

    @pl.loop(0, 8)
    def _(i):
        pltpu.make_async_copy(posall.at[i], posall.at[i], qr.at[i]).wait()
    table = posall[...].reshape(128, 128)
    pick = onehot(iota((8, 128), 1) == me * 8 + iota((8, 128), 0))
    digits = [dot_nt(pick, part.astype(f32).astype(BF16)).astype(BF16) for part in (table >> 5, table & 31)]
    n = iota((128, 512), 1)
    spread = onehot(iota((128, 512), 0) == ((n >> 2) & 7) * 16 + (n >> 5))
    full = dot(digits[0], spread) * 32.0 + dot(digits[1], spread)
    sub, lane = iota((8, 512), 0), iota((8, 512), 1)
    wants = []
    for h in range(2):
        want = jnp.sum(jnp.where(sub == h * 4 + (lane & 3), full, 0.0), axis=0, keepdims=True)
        wants.append(want.astype(jnp.int32))

    @pl.loop(0, 8)
    def _(i):
        pltpu.make_async_copy(mid2.at[i], mid2.at[i], c1r.at[i]).wait()

    def back_z(i):
        zz = lax.rem(z + i, NZ)
        return pltpu.make_async_remote_copy(
            src_ref=mid2.at[:, zz], dst_ref=back.at[z], send_sem=c2s.at[i], recv_sem=c2r.at[i],
            device_id=dev(y, zz, k, c), device_id_type=MESH)

    @pl.loop(1, NZ)
    def _(i):
        back_z(i).start()
    own_back = pltpu.make_async_copy(mid2.at[:, z], back.at[z], c2r.at[0])
    own_back.start()
    for h in range(2):
        placing[h] = onehot(iota((1024, 512), 0) == wants[h])

    for a in range(4):
        for i in range(1, 4):
            weight_x(a, i).wait_send()
            weight_core(a, i).wait_send()

    @pl.loop(1, NZ)
    def _(j):
        rows_z(j).wait_send()
        pos_z(j).wait_send()

    @pl.loop(0, 8)
    def _(i):
        @pl.when(jnp.logical_not(is_me(i)))
        def _():
            pos_on(i).wait_send()
            back_xy(i).wait_send()
            for g in range(8):
                on(g, i).wait_send()
    own_back.wait()

    @pl.loop(1, NZ)
    def _(i):
        back_z(i).wait()
    got = jnp.transpose(back[...].astype(f32).reshape(512, 128)).astype(BF16)
    result_t[...] = (dot_nt(got[:64], placing[0]) + dot_nt(got[64:], placing[1])).astype(BF16)


def shards(raw_points, cell_ids, row_counts, hilbert_position, z_position,
           pool_weight, qkv_weight, proj_weight, fc1_weight, fc2_weight):
    S, V, I32 = jax.ShapeDtypeStruct, pltpu.VMEM, jnp.int32

    def sems(*shape):
        return pltpu.SemaphoreType.DMA(shape)
    out = pl.pallas_call(
        layer_kernel,
        out_shape=S((64, 1024), BF16),
        in_specs=[ANY] * 10,
        out_specs=VM,
        scratch_shapes=[
            V((3072, 128), BF16), V((24, 128), I32), V((1, 2048), I32), V((8, 128), I32), V((1, 128), I32),
            V((128, 256), BF16), V((4, 3, 64, 256), BF16), V((4, 64, 256), BF16), V((4, 256, 256), BF16),
            V((4, 256, 256), BF16),
            V((NZ, 2, 16, 128), BF16), V((NZ, 1, 128), I32), V((NZ, 1, 128), I32), V((8, NZ, 1, 128), I32),
            V((NZ, 2, 16, 128), BF16), V((NZ, 8, 16, 128), BF16), V((1024, 128), jnp.float32),
            V((2, 4, NZ, 4, 128), BF16), V((8, NZ, 4, 128), BF16),
            sems(10), sems(NZ), sems(NZ), sems(NZ), sems(NZ), sems(8, 8), sems(8, 8),
            sems(4, 4), sems(4, 4), sems(4, 4), sems(4, 4), sems(8), sems(8), sems(8), sems(8), sems(NZ), sems(NZ),
            V((NZ, 8, 4, 128), BF16), V((2, 1024, 512), BF16),
        ],
        compiler_params=pltpu.CompilerParams(collective_id=0, has_side_effects=True,
                                             vmem_limit_bytes=LIMIT),
        name="layer",
    )(raw_points, cell_ids.reshape(24, 128), hilbert_position, z_position.reshape(8, 128),
      row_counts.reshape(1, 128), pool_weight, jnp.transpose(qkv_weight, (0, 2, 1)), proj_weight.T,
      fc1_weight, fc2_weight)
    return out.T


def solution(mesh):
    in_specs = (P("pts", None), P("pts"), P(), P("pts", None), P("pts"), P(),
                P(None, None, "ch"), P(None, "ch"), P(None, "ch"), P("ch", None))
    return jax.shard_map(shards, mesh=mesh, in_specs=in_specs, out_specs=P("pts", "ch"),
                         check_vma=False)
```

```python
import jax
import jax.numpy as jnp
from jax import lax
from jax.experimental import pallas as pl
from jax.experimental.pallas import tpu as pltpu
from jax.sharding import PartitionSpec as P

BF16 = jnp.bfloat16
EPS = 1e-5


def iota(shape, dim):
    return lax.broadcasted_iota(jnp.int32, shape, dim)


def dot(a, b):
    return jnp.dot(a, b, preferred_element_type=jnp.float32)


def dot_nt(a, b):
    return lax.dot_general(a, b, (((1,), (1,)), ((), ())), preferred_element_type=jnp.float32)


def onehot(mask):
    return jnp.where(mask, 1.0, 0.0).astype(BF16)


def row_norm(values):
    center = values - jnp.mean(values, axis=-1, keepdims=True)
    spread = jnp.mean(center * center, axis=-1, keepdims=True)
    return (center * lax.rsqrt(spread + EPS)).astype(BF16)


MESH = pl.DeviceIdType.MESH
NZ = 16
LIMIT = 64 * 1024 * 1024 - 65536
ANY = pl.BlockSpec(memory_space=pltpu.HBM)
VM = pl.BlockSpec(memory_space=pltpu.VMEM)


def place():
    p, c = lax.axis_index("pts"), lax.axis_index("ch")
    return p // 32, lax.rem(p // 2, NZ), lax.rem(p, 2), c


def dev(y, z, k, c):
    return (y * 32 + z * 2 + k, c)


def hop(j):
    return lax.rem(j, 2) * ((j + 1) // 2) + (1 - lax.rem(j, 2)) * (NZ - j // 2)


def layer_kernel(raw_h, ids_h, hilbert_h, zpos_h, counts_h, pool_h, qkv_h, proj_h, fc1_h, fc2_h,
                 result_t,
                 raw, ids, hilbert, zpos, counts, pool, wq, wp, w1, w2,
                 slots, pos, posz, posall, mid, rows, acc, out, mid2,
                 lsem, ps, pr, s2, r2, s3, r3, ws, wr, fs, fr, qs, qr, c1s, c1r, c2s, c2r, back, placing):
    y, z, k, c = place()
    me = y * 2 + k
    f32 = jnp.float32
    on_diag = y == c
    barrier = pltpu.get_barrier_semaphore()

    def hello(d):
        pl.semaphore_signal(barrier, inc=1, device_id=d, device_id_type=MESH)

    hello(dev(y, z, 1 - k, c))
    for i in range(1, 4):
        hello(dev(y, z, k, lax.rem(c + i, 4)))

    @pl.loop(1, NZ)
    def _(i):
        hello(dev(y, lax.rem(z + i, NZ), k, c))

    @pl.loop(0, 8)
    def _(i):
        @pl.when(jnp.logical_not(on_diag & (i == me)))
        def _():
            hello(dev(i // 2, z, lax.rem(i, 2), y))

    loads = [pltpu.make_async_copy(a, b, lsem.at[i]) for i, (a, b) in enumerate((
        (hilbert_h, hilbert), (zpos_h, zpos), (ids_h, ids), (raw_h, raw), (counts_h, counts), (pool_h, pool),
        (qkv_h, wq.at[c]), (proj_h, wp.at[c]), (fc1_h, w1.at[c]), (fc2_h, w2.at[c])))]
    for load in loads:
        load.start()

    loads[0].wait()
    target = hilbert[...]
    rel = jnp.where(target >= 0, (target >> 10) - c * 32, -1)
    hot = onehot(iota((32, 2048), 0) == rel)
    upper = onehot(iota((256, 256), 0) < iota((256, 256), 1))
    before = jnp.zeros((32, 1), f32)
    cell = jnp.zeros((512, 256), f32)
    for b in range(8):
        part = hot[:, b * 256:(b + 1) * 256]
        part32 = part.astype(f32)
        rank = jnp.sum((dot(part, upper) + before) * part32, axis=0, keepdims=True)
        before = before + jnp.sum(part32, axis=1, keepdims=True)
        r = rel[:, b * 256:(b + 1) * 256]
        index = jnp.where((r >= 0) & (r < 32), r * 16 + rank.astype(jnp.int32), -1)
        number = jnp.where(iota((256, 256), 1) >= 128, iota((256, 256), 0), b)
        cell = cell + dot(onehot(iota((512, 256), 0) == index), number.astype(f32).astype(BF16))
    cell = cell[:, :128] * 256.0 + cell[:, 128:]

    @pl.when(on_diag)
    def _():
        pl.semaphore_wait(barrier, 26)

    @pl.when(jnp.logical_not(on_diag))
    def _():
        pl.semaphore_wait(barrier, 27)

    def parts(a):
        return ((qkv_h, wq, 32, True), (fc1_h, w1, 128, False), (proj_h, wp, 32, False),
                (fc2_h, w2, 128, False))[a]

    def weight_x(a, i):
        src, dst, size, deep = parts(a)
        half = pl.ds(pl.multiple_of(k * size, size), size)
        return pltpu.make_async_remote_copy(
            src_ref=src.at[:, half] if deep else src.at[half],
            dst_ref=dst.at[c, :, half] if deep else dst.at[c, half],
            send_sem=ws.at[a, i], recv_sem=wr.at[a, i],
            device_id=dev(y, z, k, lax.rem(c + i, 4)), device_id_type=MESH)

    def weight_core(a, i):
        _, dst, size, deep = parts(a)
        half = pl.ds(pl.multiple_of(k * size, size), size)
        owner = lax.rem(c - i + 4, 4)
        at = dst.at[owner, :, half] if deep else dst.at[owner, half]
        return pltpu.make_async_remote_copy(
            src_ref=at, dst_ref=at, send_sem=fs.at[a, i], recv_sem=fr.at[a, i],
            device_id=dev(y, z, 1 - k, c), device_id_type=MESH)

    for i in range(1, 4):
        weight_x(0, i).start()

    loads[2].wait()
    loads[3].wait()
    total = jnp.zeros((512, 256), f32)
    one = jnp.ones((512, 128), BF16)
    points = ids[...].astype(f32)
    for b in range(6):
        member = jnp.concatenate(
            [onehot(cell == points[4 * b + j:4 * b + j + 1]) for j in range(4)], axis=1)
        total = total + dot(member, jnp.concatenate([raw[b * 512:(b + 1) * 512], one], axis=1))
    mean = (total[:, :128] / total[:, 128:]).astype(BF16)
    for zz in range(NZ):
        for kk in range(2):
            slots[zz, kk] = mean[zz * 32 + kk * 16:zz * 32 + kk * 16 + 16]

    def rows_z(j):
        zz = lax.rem(z + hop(j), NZ)
        return pltpu.make_async_remote_copy(
            src_ref=slots.at[zz], dst_ref=mid.at[j], send_sem=s2.at[j], recv_sem=r2.at[j],
            device_id=dev(y, zz, k, c), device_id_type=MESH)

    @pl.loop(1, NZ)
    def _(j):
        rows_z(NZ - j).start()
    own_z = pltpu.make_async_copy(slots.at[z], mid.at[0], r2.at[0])
    own_z.start()

    def is_me(i):
        return on_diag & (i == c * 2 + k)

    def on(g, i):
        kk, cc = lax.rem(i, 2), i // 2
        return pltpu.make_async_remote_copy(
            src_ref=mid.at[2 * g:2 * g + 2, kk], dst_ref=rows.at[2 * g:2 * g + 2, me],
            send_sem=s3.at[g, i], recv_sem=r3.at[g, me],
            device_id=dev(c, z, kk, cc), device_id_type=MESH)

    def on_start(g):
        @pl.loop(0, 8)
        def _(i):
            @pl.when(is_me(i))
            def _():
                pltpu.make_async_copy(mid.at[2 * g:2 * g + 2, k], rows.at[2 * g:2 * g + 2, me],
                                      r3.at[g, me]).start()

            @pl.when(jnp.logical_not(is_me(i)))
            def _():
                on(g, i).start()

    def on_arrived(g):
        @pl.loop(0, 8)
        def _(i):
            block = rows.at[2 * g:2 * g + 2, i]
            pltpu.make_async_copy(block, block, r3.at[g, i]).wait()

    loads[1].wait()
    z_rows = zpos[...]
    z32 = z_rows.astype(f32)
    column = jnp.concatenate(
        [jnp.transpose(jnp.broadcast_to(z32[j:j + 1], (128, 128))) for j in range(8)], axis=0)
    split = jnp.zeros((32, 128), f32)
    for j in range(8):
        rank = jnp.sum(jnp.where(column < z32[j:j + 1], 1.0, 0.0), axis=0, keepdims=True)
        rank = rank.astype(jnp.int32)
        own = z_rows[j:j + 1] & 1023
        dest = rank >> 3
        lane = ((dest >> 5) * 2 + (dest & 1)) * 8 + (rank & 7)
        sub = iota((32, 128), 0)
        digit = jnp.where(sub < 16, own >> 5, own & 31).astype(f32)
        left = jnp.where((sub & 15) == ((dest >> 1) & 15), digit, 0.0).astype(BF16)
        split = split + dot_nt(left, onehot(iota((128, 128), 0) == lane))
    table = (split[:16] * 32.0 + split[16:]).astype(jnp.int32)
    for zz in range(NZ):
        pos[zz] = table[zz:zz + 1]

    def pos_z(j):
        zz = lax.rem(z + j, NZ)
        return pltpu.make_async_remote_copy(
            src_ref=pos.at[zz], dst_ref=posz.at[z], send_sem=ps.at[j], recv_sem=pr.at[j],
            device_id=dev(y, zz, k, c), device_id_type=MESH)

    def pos_arrived(j):
        zs = lax.rem(z - j + NZ, NZ)
        return pltpu.make_async_copy(posz.at[zs], posz.at[zs], pr.at[j])

    own_pos = pltpu.make_async_copy(pos.at[z], posz.at[z], pr.at[0])
    own_pos.start()

    loads[4].wait()
    units = jnp.broadcast_to((counts[...] >> 7).astype(f32).astype(BF16), (8, 128))
    col = iota((128, 2048), 1)
    hop_no, from_yc = col >> 7, (col >> 4) & 7
    away = jnp.where((hop_no & 1) == 1, (hop_no + 1) >> 1, NZ - (hop_no >> 1))
    source = (from_yc >> 1) * 32 + ((z + NZ - away) & 15) * 2 + (from_yc & 1)
    held = dot(units, onehot(iota((128, 2048), 0) == source))[:1].astype(jnp.int32)
    first = dot(units, onehot(iota((128, 2048), 0) < source))[:1].astype(jnp.int32)
    within = iota((1, 2048), 1) & 15
    order = jnp.where(within < held, first + within, -1)

    def gather_group(g):
        on_arrived(g)
        sel = onehot(iota((1024, 256), 0) == order[:, g * 256:(g + 1) * 256])
        piece = dot(sel, rows[2 * g:2 * g + 2].reshape(256, 128))
        if g == 0:
            acc[...] = piece
        else:
            acc[...] += piece

    for g in range(8):
        for j in (2 * g, 2 * g + 1):
            pltpu.make_async_copy(mid.at[j], mid.at[j], r2.at[j]).wait()
        on_start(g)
        if g == 0:
            @pl.loop(1, NZ)
            def _(j):
                pos_z(j).start()
    for a in range(1, 4):
        for i in range(1, 4):
            weight_x(a, i).start()
    for i in range(1, 4):
        weight_x(0, i).wait_recv()
        weight_core(0, i).start()
    for g in range(8):
        gather_group(g)

    @pl.loop(0, NZ)
    def _(j):
        pos_arrived(j).wait()

    def pos_on(i):
        return pltpu.make_async_remote_copy(
            src_ref=posz, dst_ref=posall.at[me], send_sem=qs.at[i], recv_sem=qr.at[me],
            device_id=dev(c, z, lax.rem(i, 2), i // 2), device_id_type=MESH)

    @pl.loop(0, 8)
    def _(i):
        @pl.when(is_me(i))
        def _():
            pltpu.make_async_copy(posz, posall.at[me], qr.at[me]).start()

        @pl.when(jnp.logical_not(is_me(i)))
        def _():
            pos_on(i).start()

    x = acc[...].astype(BF16)
    loads[5].wait()
    w = pool[...]
    normed = row_norm(dot(x, w).astype(BF16).astype(f32))
    t = iota((256, 256), 0)
    hop_no = 15 - ((t >> 7) * 8 + ((t >> 2) & 7))
    away = jnp.where((hop_no & 1) == 1, (hop_no + 1) >> 1, NZ - (hop_no >> 1))
    row = 8 * (((z + away) & 15) * 2 + ((t >> 5) & 1)) + 4 * ((t >> 6) & 1) + (t & 3)
    quarter = acc[pl.ds(pl.multiple_of(c * 256, 256), 256)].astype(BF16)
    mine = dot(onehot(iota((256, 256), 1) == row), quarter)
    features = dot(mine.astype(BF16), w).astype(BF16).astype(f32)
    loads[6].wait()
    for i in range(1, 4):
        weight_core(0, i).wait_recv()
    keys = dot_nt(wq[:, 1].reshape(256, 256), normed).astype(BF16)
    values = dot_nt(normed, wq[:, 2].reshape(256, 256)).astype(BF16)
    query = dot_nt(row_norm(features), wq[:, 0].reshape(256, 256)).astype(BF16).astype(f32)
    head_of = iota((256, 256), 1) >> 4
    ones = jnp.ones((1024, 128), BF16)
    summed = [jnp.concatenate([values[:, u * 128:(u + 1) * 128], ones], axis=1) for u in range(2)]
    scale = 0.25 * 1.4426950408889634

    def score(h):
        return dot(jnp.where(head_of == h, query, 0.0).astype(BF16), keys)

    lane_head = iota((256, 128), 1) >> 4
    sides = [jnp.zeros((256, 128), f32)] * 2
    scores = score(0)
    for h in range(16):
        later = score(h + 1) if h < 15 else None
        if h == 12:
            for a in range(1, 4):
                for i in range(1, 4):
                    weight_x(a, i).wait_recv()
                    weight_core(a, i).start()
        peak = jnp.max(scores, axis=1, keepdims=True)
        mix = dot(jnp.exp2((scores - peak) * scale).astype(BF16), summed[h // 8])
        sides[h // 8] = jnp.where(lane_head == h % 8, mix[:, :128] / mix[:, 128:], sides[h // 8])
        scores = later
    attended = jnp.concatenate(sides, axis=1).astype(BF16)
    for load in loads[7:]:
        load.wait()
    for a in range(1, 4):
        for i in range(1, 4):
            weight_core(a, i).wait_recv()
    middle = (features + dot_nt(attended, wp[...].reshape(256, 256))).astype(BF16).astype(f32)

    def back_xy(q, i):
        kk, cc = lax.rem(i, 2), i // 2
        return pltpu.make_async_remote_copy(
            src_ref=out.at[q, kk, cc], dst_ref=mid2.at[q, me], send_sem=c1s.at[q, i], recv_sem=c1r.at[q, me],
            device_id=dev(c, z, kk, cc), device_id_type=MESH)

    def forward(q):
        part = middle[q * 128:(q + 1) * 128]
        normed2 = row_norm(part)
        for i in range(4):
            v = dot(normed2, w1[i])
            hidden = (v * (1.0 + lax.erf(v * 0.7071067811865476)) * 0.5).astype(BF16)
            part = part + dot(hidden, w2[i])
        for kk in range(2):
            for cc in range(4):
                both = [part[h * 64 + kk * 32:h * 64 + kk * 32 + 32, cc * 64:cc * 64 + 64] for h in range(2)]
                out[q, kk, cc] = jnp.concatenate(both, axis=1).reshape(8, 4, 128).astype(BF16)

        @pl.loop(0, 8)
        def _(i):
            @pl.when(is_me(i))
            def _():
                pltpu.make_async_copy(out.at[q, k, c], mid2.at[q, me], c1r.at[q, me]).start()

            @pl.when(jnp.logical_not(is_me(i)))
            def _():
                back_xy(q, i).start()

    def back_z(j):
        zz = lax.rem(z + hop(j), NZ)
        at = NZ - 1 - j
        return pltpu.make_async_remote_copy(
            src_ref=mid2.at[at // 8, :, lax.rem(at, 8)], dst_ref=back.at[z], send_sem=c2s.at[j],
            recv_sem=c2r.at[j], device_id=dev(y, zz, k, c), device_id_type=MESH)

    def middle_arrived(q):
        @pl.loop(0, 8)
        def _(i):
            pltpu.make_async_copy(mid2.at[q, i], mid2.at[q, i], c1r.at[q, i]).wait()

    forward(0)
    forward(1)
    middle_arrived(0)

    @pl.loop(0, 8)
    def _(i):
        back_z(NZ - 1 - i).start()

    @pl.loop(0, 8)
    def _(i):
        pltpu.make_async_copy(posall.at[i], posall.at[i], qr.at[i]).wait()
    table = posall[...].reshape(128, 128)
    pick = onehot(iota((8, 128), 1) == me * 8 + iota((8, 128), 0))
    digits = [dot_nt(pick, part.astype(f32).astype(BF16)).astype(BF16) for part in (table >> 5, table & 31)]
    n = iota((128, 512), 1)
    spread = onehot(iota((128, 512), 0) == ((n >> 2) & 7) * 16 + (n >> 5))
    full = dot(digits[0], spread) * 32.0 + dot(digits[1], spread)
    sub, lane = iota((8, 512), 0), iota((8, 512), 1)
    wants = []
    for h in range(2):
        want = jnp.sum(jnp.where(sub == h * 4 + (lane & 3), full, 0.0), axis=0, keepdims=True)
        wants.append(want.astype(jnp.int32))

    middle_arrived(1)

    @pl.loop(8, NZ - 1)
    def _(i):
        back_z(NZ - 1 - i).start()
    own_back = pltpu.make_async_copy(mid2.at[1, :, 7], back.at[z], c2r.at[0])
    own_back.start()
    for h in range(2):
        placing[h] = onehot(iota((1024, 512), 0) == wants[h])

    for a in range(4):
        for i in range(1, 4):
            weight_x(a, i).wait_send()
            weight_core(a, i).wait_send()

    @pl.loop(1, NZ)
    def _(j):
        rows_z(j).wait_send()
        pos_z(j).wait_send()

    @pl.loop(0, 8)
    def _(i):
        @pl.when(jnp.logical_not(is_me(i)))
        def _():
            pos_on(i).wait_send()
            back_xy(0, i).wait_send()
            back_xy(1, i).wait_send()
            for g in range(8):
                on(g, i).wait_send()
    own_back.wait()

    @pl.loop(1, NZ)
    def _(i):
        back_z(i).wait()
    got = jnp.transpose(back[...].astype(f32).reshape(512, 128)).astype(BF16)
    result_t[...] = (dot_nt(got[:64], placing[0]) + dot_nt(got[64:], placing[1])).astype(BF16)


def shards(raw_points, cell_ids, row_counts, hilbert_position, z_position,
           pool_weight, qkv_weight, proj_weight, fc1_weight, fc2_weight):
    S, V, I32 = jax.ShapeDtypeStruct, pltpu.VMEM, jnp.int32

    def sems(*shape):
        return pltpu.SemaphoreType.DMA(shape)
    out = pl.pallas_call(
        layer_kernel,
        out_shape=S((64, 1024), BF16),
        in_specs=[ANY] * 10,
        out_specs=VM,
        scratch_shapes=[
            V((3072, 128), BF16), V((24, 128), I32), V((1, 2048), I32), V((8, 128), I32), V((1, 128), I32),
            V((128, 256), BF16), V((4, 3, 64, 256), BF16), V((4, 64, 256), BF16), V((4, 256, 256), BF16),
            V((4, 256, 256), BF16),
            V((NZ, 2, 16, 128), BF16), V((NZ, 1, 128), I32), V((NZ, 1, 128), I32), V((8, NZ, 1, 128), I32),
            V((NZ, 2, 16, 128), BF16), V((NZ, 8, 16, 128), BF16), V((1024, 128), jnp.float32),
            V((2, 2, 4, 8, 4, 128), BF16), V((2, 8, 8, 4, 128), BF16),
            sems(10), sems(NZ), sems(NZ), sems(NZ), sems(NZ), sems(8, 8), sems(8, 8),
            sems(4, 4), sems(4, 4), sems(4, 4), sems(4, 4), sems(8), sems(8), sems(2, 8), sems(2, 8), sems(NZ), sems(NZ),
            V((NZ, 8, 4, 128), BF16), V((2, 1024, 512), BF16),
        ],
        compiler_params=pltpu.CompilerParams(collective_id=0, has_side_effects=True,
                                             vmem_limit_bytes=LIMIT),
        name="layer",
    )(raw_points, cell_ids.reshape(24, 128), hilbert_position, z_position.reshape(8, 128),
      row_counts.reshape(1, 128), pool_weight, jnp.transpose(qkv_weight, (0, 2, 1)), proj_weight.T,
      fc1_weight, fc2_weight)
    return out.T


def solution(mesh):
    in_specs = (P("pts", None), P("pts"), P(), P("pts", None), P("pts"), P(),
                P(None, None, "ch"), P(None, "ch"), P(None, "ch"), P("ch", None))
    return jax.shard_map(shards, mesh=mesh, in_specs=in_specs, out_specs=P("pts", "ch"),
                         check_vma=False)
```

```python
import jax
import jax.numpy as jnp
from jax import lax
from jax.experimental import pallas as pl
from jax.experimental.pallas import tpu as pltpu
from jax.sharding import PartitionSpec as P

BF16 = jnp.bfloat16
EPS = 1e-5


def iota(shape, dim):
    return lax.broadcasted_iota(jnp.int32, shape, dim)


def dot(a, b):
    return jnp.dot(a, b, preferred_element_type=jnp.float32)


def dot_nt(a, b):
    return lax.dot_general(a, b, (((1,), (1,)), ((), ())), preferred_element_type=jnp.float32)


def onehot(mask):
    return jnp.where(mask, 1.0, 0.0).astype(BF16)


def row_norm(values):
    center = values - jnp.mean(values, axis=-1, keepdims=True)
    spread = jnp.mean(center * center, axis=-1, keepdims=True)
    return (center * lax.rsqrt(spread + EPS)).astype(BF16)


MESH = pl.DeviceIdType.MESH
NZ = 16
LIMIT = 64 * 1024 * 1024 - 65536
ANY = pl.BlockSpec(memory_space=pltpu.HBM)
VM = pl.BlockSpec(memory_space=pltpu.VMEM)


def place():
    p, c = lax.axis_index("pts"), lax.axis_index("ch")
    return p // 32, lax.rem(p // 2, NZ), lax.rem(p, 2), c


def dev(y, z, k, c):
    return (y * 32 + z * 2 + k, c)


def hop(j):
    return lax.rem(j, 2) * ((j + 1) // 2) + (1 - lax.rem(j, 2)) * (NZ - j // 2)


def layer_kernel(raw_h, ids_h, hilbert_h, zpos_h, counts_h, pool_h, qkv_h, proj_h, fc1_h, fc2_h,
                 result_t,
                 raw, ids, hilbert, zpos, counts, pool, wq, wp, w1, w2,
                 slots, pos, posz, posall, mid, rows, acc, out, mid2,
                 lsem, ps, pr, s2, r2, s3, r3, ws, wr, fs, fr, qs, qr, c1s, c1r, c2s, c2r, back, placing):
    y, z, k, c = place()
    me = y * 2 + k
    f32 = jnp.float32
    on_diag = y == c
    barrier = pltpu.get_barrier_semaphore()

    def hello(d):
        pl.semaphore_signal(barrier, inc=1, device_id=d, device_id_type=MESH)

    loads = [pltpu.make_async_copy(a, b, lsem.at[i]) for i, (a, b) in enumerate((
        (hilbert_h, hilbert), (zpos_h, zpos), (ids_h, ids), (raw_h, raw), (counts_h, counts), (pool_h, pool),
        (qkv_h, wq.at[c]), (proj_h, wp.at[c]), (fc1_h, w1.at[c]), (fc2_h, w2.at[c])))]
    for load in loads:
        load.start()

    hello(dev(y, z, 1 - k, c))
    for i in range(1, 4):
        hello(dev(y, z, k, lax.rem(c + i, 4)))

    @pl.loop(1, NZ)
    def _(i):
        hello(dev(y, lax.rem(z + i, NZ), k, c))

    @pl.loop(0, 8)
    def _(i):
        @pl.when(jnp.logical_not(on_diag & (i == me)))
        def _():
            hello(dev(i // 2, z, lax.rem(i, 2), y))

    loads[0].wait()
    target = hilbert[...]
    rel = jnp.where(target >= 0, (target >> 10) - c * 32, -1)
    hot = onehot(iota((32, 2048), 0) == rel)
    upper = onehot(iota((256, 256), 0) < iota((256, 256), 1))
    before = jnp.zeros((32, 1), f32)
    cell = jnp.zeros((512, 256), f32)
    for b in range(8):
        part = hot[:, b * 256:(b + 1) * 256]
        part32 = part.astype(f32)
        rank = jnp.sum((dot(part, upper) + before) * part32, axis=0, keepdims=True)
        before = before + jnp.sum(part32, axis=1, keepdims=True)
        r = rel[:, b * 256:(b + 1) * 256]
        index = jnp.where((r >= 0) & (r < 32), r * 16 + rank.astype(jnp.int32), -1)
        number = jnp.where(iota((256, 256), 1) >= 128, iota((256, 256), 0), b)
        cell = cell + dot(onehot(iota((512, 256), 0) == index), number.astype(f32).astype(BF16))
    cell = cell[:, :128] * 256.0 + cell[:, 128:]

    @pl.when(on_diag)
    def _():
        pl.semaphore_wait(barrier, 26)

    @pl.when(jnp.logical_not(on_diag))
    def _():
        pl.semaphore_wait(barrier, 27)

    def parts(a):
        return ((qkv_h, wq, 32, True), (fc1_h, w1, 128, False), (proj_h, wp, 32, False),
                (fc2_h, w2, 128, False))[a]

    def weight_x(a, i):
        src, dst, size, deep = parts(a)
        half = pl.ds(pl.multiple_of(k * size, size), size)
        return pltpu.make_async_remote_copy(
            src_ref=src.at[:, half] if deep else src.at[half],
            dst_ref=dst.at[c, :, half] if deep else dst.at[c, half],
            send_sem=ws.at[a, i], recv_sem=wr.at[a, i],
            device_id=dev(y, z, k, lax.rem(c + i, 4)), device_id_type=MESH)

    def weight_core(a, i):
        _, dst, size, deep = parts(a)
        half = pl.ds(pl.multiple_of(k * size, size), size)
        owner = lax.rem(c - i + 4, 4)
        at = dst.at[owner, :, half] if deep else dst.at[owner, half]
        return pltpu.make_async_remote_copy(
            src_ref=at, dst_ref=at, send_sem=fs.at[a, i], recv_sem=fr.at[a, i],
            device_id=dev(y, z, 1 - k, c), device_id_type=MESH)

    for i in range(1, 4):
        weight_x(0, i).start()

    loads[2].wait()
    loads[3].wait()
    total = jnp.zeros((512, 256), f32)
    one = jnp.ones((512, 128), BF16)
    points = ids[...].astype(f32)
    for b in range(6):
        member = jnp.concatenate(
            [onehot(cell == points[4 * b + j:4 * b + j + 1]) for j in range(4)], axis=1)
        total = total + dot(member, jnp.concatenate([raw[b * 512:(b + 1) * 512], one], axis=1))
    mean = (total[:, :128] / total[:, 128:]).astype(BF16)
    for zz in range(NZ):
        for kk in range(2):
            slots[zz, kk] = mean[zz * 32 + kk * 16:zz * 32 + kk * 16 + 16]

    def rows_z(j):
        zz = lax.rem(z + hop(j), NZ)
        return pltpu.make_async_remote_copy(
            src_ref=slots.at[zz], dst_ref=mid.at[j], send_sem=s2.at[j], recv_sem=r2.at[j],
            device_id=dev(y, zz, k, c), device_id_type=MESH)

    @pl.loop(1, NZ)
    def _(j):
        rows_z(NZ - j).start()
    own_z = pltpu.make_async_copy(slots.at[z], mid.at[0], r2.at[0])
    own_z.start()

    def is_me(i):
        return on_diag & (i == c * 2 + k)

    def on(g, i):
        kk, cc = lax.rem(i, 2), i // 2
        return pltpu.make_async_remote_copy(
            src_ref=mid.at[4 * g:4 * g + 4, kk], dst_ref=rows.at[4 * g:4 * g + 4, me],
            send_sem=s3.at[g, i], recv_sem=r3.at[g, me],
            device_id=dev(c, z, kk, cc), device_id_type=MESH)

    def on_start(g):
        @pl.loop(0, 8)
        def _(i):
            @pl.when(is_me(i))
            def _():
                pltpu.make_async_copy(mid.at[4 * g:4 * g + 4, k], rows.at[4 * g:4 * g + 4, me],
                                      r3.at[g, me]).start()

            @pl.when(jnp.logical_not(is_me(i)))
            def _():
                on(g, i).start()

    def on_arrived(g):
        @pl.loop(0, 8)
        def _(i):
            block = rows.at[4 * g:4 * g + 4, i]
            pltpu.make_async_copy(block, block, r3.at[g, i]).wait()

    loads[1].wait()
    z_rows = zpos[...]
    z32 = z_rows.astype(f32)
    column = jnp.concatenate(
        [jnp.transpose(jnp.broadcast_to(z32[j:j + 1], (128, 128))) for j in range(8)], axis=0)
    split = jnp.zeros((32, 128), f32)
    for j in range(8):
        rank = jnp.sum(jnp.where(column < z32[j:j + 1], 1.0, 0.0), axis=0, keepdims=True)
        rank = rank.astype(jnp.int32)
        own = z_rows[j:j + 1] & 1023
        dest = rank >> 3
        lane = ((dest >> 5) * 2 + (dest & 1)) * 8 + (rank & 7)
        sub = iota((32, 128), 0)
        digit = jnp.where(sub < 16, own >> 5, own & 31).astype(f32)
        left = jnp.where((sub & 15) == ((dest >> 1) & 15), digit, 0.0).astype(BF16)
        split = split + dot_nt(left, onehot(iota((128, 128), 0) == lane))
    table = (split[:16] * 32.0 + split[16:]).astype(jnp.int32)
    for zz in range(NZ):
        pos[zz] = table[zz:zz + 1]

    def pos_z(j):
        zz = lax.rem(z + j, NZ)
        return pltpu.make_async_remote_copy(
            src_ref=pos.at[zz], dst_ref=posz.at[z], send_sem=ps.at[j], recv_sem=pr.at[j],
            device_id=dev(y, zz, k, c), device_id_type=MESH)

    def pos_arrived(j):
        zs = lax.rem(z - j + NZ, NZ)
        return pltpu.make_async_copy(posz.at[zs], posz.at[zs], pr.at[j])

    own_pos = pltpu.make_async_copy(pos.at[z], posz.at[z], pr.at[0])
    own_pos.start()

    loads[4].wait()
    units = jnp.broadcast_to((counts[...] >> 7).astype(f32).astype(BF16), (8, 128))
    col = iota((128, 2048), 1)
    hop_no, from_yc = col >> 7, (col >> 4) & 7
    away = jnp.where((hop_no & 1) == 1, (hop_no + 1) >> 1, NZ - (hop_no >> 1))
    source = (from_yc >> 1) * 32 + ((z + NZ - away) & 15) * 2 + (from_yc & 1)
    held = dot(units, onehot(iota((128, 2048), 0) == source))[:1].astype(jnp.int32)
    first = dot(units, onehot(iota((128, 2048), 0) < source))[:1].astype(jnp.int32)
    within = iota((1, 2048), 1) & 15
    order = jnp.where(within < held, first + within, -1)

    def gather_group(g):
        on_arrived(g)
        sel = onehot(iota((1024, 512), 0) == order[:, g * 512:(g + 1) * 512])
        piece = dot(sel, rows[4 * g:4 * g + 4].reshape(512, 128))
        if g == 0:
            acc[...] = piece
        else:
            acc[...] += piece

    for g in range(4):
        for j in range(4 * g, 4 * g + 4):
            pltpu.make_async_copy(mid.at[j], mid.at[j], r2.at[j]).wait()
        on_start(g)
        if g == 0:
            @pl.loop(1, NZ)
            def _(j):
                pos_z(j).start()
    for a in range(1, 4):
        for i in range(1, 4):
            weight_x(a, i).start()
    for i in range(1, 4):
        weight_x(0, i).wait_recv()
        weight_core(0, i).start()
    for g in range(4):
        gather_group(g)

    @pl.loop(0, NZ)
    def _(j):
        pos_arrived(j).wait()

    def pos_on(i):
        return pltpu.make_async_remote_copy(
            src_ref=posz, dst_ref=posall.at[me], send_sem=qs.at[i], recv_sem=qr.at[me],
            device_id=dev(c, z, lax.rem(i, 2), i // 2), device_id_type=MESH)

    @pl.loop(0, 8)
    def _(i):
        @pl.when(is_me(i))
        def _():
            pltpu.make_async_copy(posz, posall.at[me], qr.at[me]).start()

        @pl.when(jnp.logical_not(is_me(i)))
        def _():
            pos_on(i).start()

    x = acc[...].astype(BF16)
    loads[5].wait()
    w = pool[...]
    normed = row_norm(dot(x, w).astype(BF16).astype(f32))
    t = iota((256, 256), 0)
    hop_no = 15 - ((t >> 7) * 8 + ((t >> 2) & 7))
    away = jnp.where((hop_no & 1) == 1, (hop_no + 1) >> 1, NZ - (hop_no >> 1))
    row = 8 * (((z + away) & 15) * 2 + ((t >> 5) & 1)) + 4 * ((t >> 6) & 1) + (t & 3)
    quarter = acc[pl.ds(pl.multiple_of(c * 256, 256), 256)].astype(BF16)
    mine = dot(onehot(iota((256, 256), 1) == row), quarter)
    features = dot(mine.astype(BF16), w).astype(BF16).astype(f32)
    loads[6].wait()
    for i in range(1, 4):
        weight_core(0, i).wait_recv()
    keys = dot_nt(wq[:, 1].reshape(256, 256), normed).astype(BF16)
    values = dot_nt(normed, wq[:, 2].reshape(256, 256)).astype(BF16)
    query = dot_nt(row_norm(features), wq[:, 0].reshape(256, 256)).astype(BF16).astype(f32)
    head_of = iota((256, 256), 1) >> 4
    ones = jnp.ones((1024, 128), BF16)
    summed = [jnp.concatenate([values[:, u * 128:(u + 1) * 128], ones], axis=1) for u in range(2)]
    scale = 0.25 * 1.4426950408889634

    def score(h):
        return dot(jnp.where(head_of == h, query, 0.0).astype(BF16), keys)

    lane_head = iota((256, 128), 1) >> 4
    sides = [jnp.zeros((256, 128), f32)] * 2
    scores = score(0)
    for h in range(16):
        later = score(h + 1) if h < 15 else None
        if h == 12:
            for a in range(1, 4):
                for i in range(1, 4):
                    weight_x(a, i).wait_recv()
                    weight_core(a, i).start()
        peak = jnp.max(scores, axis=1, keepdims=True)
        mix = dot(jnp.exp2((scores - peak) * scale).astype(BF16), summed[h // 8])
        sides[h // 8] = jnp.where(lane_head == h % 8, mix[:, :128] / mix[:, 128:], sides[h // 8])
        scores = later
    attended = jnp.concatenate(sides, axis=1).astype(BF16)
    for load in loads[7:]:
        load.wait()
    for a in range(1, 4):
        for i in range(1, 4):
            weight_core(a, i).wait_recv()
    middle = (features + dot_nt(attended, wp[...].reshape(256, 256))).astype(BF16).astype(f32)

    def back_xy(q, i):
        kk, cc = lax.rem(i, 2), i // 2
        return pltpu.make_async_remote_copy(
            src_ref=out.at[q, kk, cc], dst_ref=mid2.at[q, me], send_sem=c1s.at[q, i], recv_sem=c1r.at[q, me],
            device_id=dev(c, z, kk, cc), device_id_type=MESH)

    def forward(q):
        part = middle[q * 128:(q + 1) * 128]
        normed2 = row_norm(part)
        for i in range(4):
            v = dot(normed2, w1[i])
            hidden = (v * (1.0 + lax.erf(v * 0.7071067811865476)) * 0.5).astype(BF16)
            part = part + dot(hidden, w2[i])
        for kk in range(2):
            for cc in range(4):
                both = [part[h * 64 + kk * 32:h * 64 + kk * 32 + 32, cc * 64:cc * 64 + 64] for h in range(2)]
                out[q, kk, cc] = jnp.concatenate(both, axis=1).reshape(8, 4, 128).astype(BF16)

        @pl.loop(0, 8)
        def _(i):
            @pl.when(is_me(i))
            def _():
                pltpu.make_async_copy(out.at[q, k, c], mid2.at[q, me], c1r.at[q, me]).start()

            @pl.when(jnp.logical_not(is_me(i)))
            def _():
                back_xy(q, i).start()

    def back_z(j):
        zz = lax.rem(z + hop(j), NZ)
        at = NZ - 1 - j
        return pltpu.make_async_remote_copy(
            src_ref=mid2.at[at // 8, :, lax.rem(at, 8)], dst_ref=back.at[z], send_sem=c2s.at[j],
            recv_sem=c2r.at[j], device_id=dev(y, zz, k, c), device_id_type=MESH)

    def middle_arrived(q):
        @pl.loop(0, 8)
        def _(i):
            pltpu.make_async_copy(mid2.at[q, i], mid2.at[q, i], c1r.at[q, i]).wait()

    forward(0)
    forward(1)
    middle_arrived(0)

    @pl.loop(0, 8)
    def _(i):
        back_z(NZ - 1 - i).start()

    @pl.loop(0, 8)
    def _(i):
        pltpu.make_async_copy(posall.at[i], posall.at[i], qr.at[i]).wait()
    table = posall[...].reshape(128, 128)
    pick = onehot(iota((8, 128), 1) == me * 8 + iota((8, 128), 0))
    digits = [dot_nt(pick, part.astype(f32).astype(BF16)).astype(BF16) for part in (table >> 5, table & 31)]
    n = iota((128, 512), 1)
    spread = onehot(iota((128, 512), 0) == ((n >> 2) & 7) * 16 + (n >> 5))
    full = dot(digits[0], spread) * 32.0 + dot(digits[1], spread)
    sub, lane = iota((8, 512), 0), iota((8, 512), 1)
    wants = []
    for h in range(2):
        want = jnp.sum(jnp.where(sub == h * 4 + (lane & 3), full, 0.0), axis=0, keepdims=True)
        wants.append(want.astype(jnp.int32))

    middle_arrived(1)

    @pl.loop(8, NZ - 1)
    def _(i):
        back_z(NZ - 1 - i).start()
    own_back = pltpu.make_async_copy(mid2.at[1, :, 7], back.at[z], c2r.at[0])
    own_back.start()
    for h in range(2):
        placing[h] = onehot(iota((1024, 512), 0) == wants[h])

    for a in range(4):
        for i in range(1, 4):
            weight_x(a, i).wait_send()
            weight_core(a, i).wait_send()

    @pl.loop(1, NZ)
    def _(j):
        rows_z(j).wait_send()
        pos_z(j).wait_send()

    @pl.loop(0, 8)
    def _(i):
        @pl.when(jnp.logical_not(is_me(i)))
        def _():
            pos_on(i).wait_send()
            back_xy(0, i).wait_send()
            back_xy(1, i).wait_send()
            for g in range(4):
                on(g, i).wait_send()
    own_back.wait()

    @pl.loop(1, NZ)
    def _(i):
        back_z(i).wait()
    got = jnp.transpose(back[...].astype(f32).reshape(512, 128)).astype(BF16)
    result_t[...] = (dot_nt(got[:64], placing[0]) + dot_nt(got[64:], placing[1])).astype(BF16)


def shards(raw_points, cell_ids, row_counts, hilbert_position, z_position,
           pool_weight, qkv_weight, proj_weight, fc1_weight, fc2_weight):
    S, V, I32 = jax.ShapeDtypeStruct, pltpu.VMEM, jnp.int32

    def sems(*shape):
        return pltpu.SemaphoreType.DMA(shape)
    out = pl.pallas_call(
        layer_kernel,
        out_shape=S((64, 1024), BF16),
        in_specs=[ANY] * 10,
        out_specs=VM,
        scratch_shapes=[
            V((3072, 128), BF16), V((24, 128), I32), V((1, 2048), I32), V((8, 128), I32), V((1, 128), I32),
            V((128, 256), BF16), V((4, 3, 64, 256), BF16), V((4, 64, 256), BF16), V((4, 256, 256), BF16),
            V((4, 256, 256), BF16),
            V((NZ, 2, 16, 128), BF16), V((NZ, 1, 128), I32), V((NZ, 1, 128), I32), V((8, NZ, 1, 128), I32),
            V((NZ, 2, 16, 128), BF16), V((NZ, 8, 16, 128), BF16), V((1024, 128), jnp.float32),
            V((2, 2, 4, 8, 4, 128), BF16), V((2, 8, 8, 4, 128), BF16),
            sems(10), sems(NZ), sems(NZ), sems(NZ), sems(NZ), sems(4, 8), sems(4, 8),
            sems(4, 4), sems(4, 4), sems(4, 4), sems(4, 4), sems(8), sems(8), sems(2, 8), sems(2, 8), sems(NZ), sems(NZ),
            V((NZ, 8, 4, 128), BF16), V((2, 1024, 512), BF16),
        ],
        compiler_params=pltpu.CompilerParams(collective_id=0, has_side_effects=True,
                                             vmem_limit_bytes=LIMIT),
        name="layer",
    )(raw_points, cell_ids.reshape(24, 128), hilbert_position, z_position.reshape(8, 128),
      row_counts.reshape(1, 128), pool_weight, jnp.transpose(qkv_weight, (0, 2, 1)), proj_weight.T,
      fc1_weight, fc2_weight)
    return out.T


def solution(mesh):
    in_specs = (P("pts", None), P("pts"), P(), P("pts", None), P("pts"), P(),
                P(None, None, "ch"), P(None, "ch"), P(None, "ch"), P("ch", None))
    return jax.shard_map(shards, mesh=mesh, in_specs=in_specs, out_specs=P("pts", "ch"),
                         check_vma=False)
```

```python
import jax
import jax.numpy as jnp
from jax import lax
from jax.experimental import pallas as pl
from jax.experimental.pallas import tpu as pltpu
from jax.sharding import PartitionSpec as P

BF16 = jnp.bfloat16
EPS = 1e-5


def iota(shape, dim):
    return lax.broadcasted_iota(jnp.int32, shape, dim)


def dot(a, b):
    return jnp.dot(a, b, preferred_element_type=jnp.float32)


def dot_nt(a, b):
    return lax.dot_general(a, b, (((1,), (1,)), ((), ())), preferred_element_type=jnp.float32)


def onehot(mask):
    return jnp.where(mask, 1.0, 0.0).astype(BF16)


def row_norm(values):
    center = values - jnp.mean(values, axis=-1, keepdims=True)
    spread = jnp.mean(center * center, axis=-1, keepdims=True)
    return (center * lax.rsqrt(spread + EPS)).astype(BF16)


MESH = pl.DeviceIdType.MESH
NZ = 16
LIMIT = 64 * 1024 * 1024 - 65536
ANY = pl.BlockSpec(memory_space=pltpu.HBM)
VM = pl.BlockSpec(memory_space=pltpu.VMEM)


def place():
    p, c = lax.axis_index("pts"), lax.axis_index("ch")
    return p // 32, lax.rem(p // 2, NZ), lax.rem(p, 2), c


def dev(y, z, k, c):
    return (y * 32 + z * 2 + k, c)


def hop(j):
    return lax.rem(j, 2) * ((j + 1) // 2) + (1 - lax.rem(j, 2)) * (NZ - j // 2)


def layer_kernel(raw_h, ids_h, hilbert_h, zpos_h, counts_h, pool_h, qkv_h, proj_h, fc1_h, fc2_h,
                 result_t,
                 raw, ids, hilbert, zpos, counts, pool, wq, wp, w1, w2,
                 slots, pos, posz, posall, mid, rows, acc, out, mid2,
                 lsem, ps, pr, s2, r2, s3, r3, ws, wr, fs, fr, qs, qr, c1s, c1r, c2s, c2r, back, placing):
    y, z, k, c = place()
    me = y * 2 + k
    f32 = jnp.float32
    on_diag = y == c
    barrier = pltpu.get_barrier_semaphore()

    def hello(d):
        pl.semaphore_signal(barrier, inc=1, device_id=d, device_id_type=MESH)

    loads = [pltpu.make_async_copy(a, b, lsem.at[i]) for i, (a, b) in enumerate((
        (hilbert_h, hilbert), (zpos_h, zpos), (ids_h, ids), (raw_h, raw), (counts_h, counts), (pool_h, pool),
        (qkv_h, wq.at[c]), (proj_h, wp.at[c]), (fc1_h, w1.at[c]), (fc2_h, w2.at[c])))]
    for load in loads:
        load.start()

    hello(dev(y, z, 1 - k, c))
    for i in range(1, 4):
        hello(dev(y, z, k, lax.rem(c + i, 4)))

    @pl.loop(1, NZ)
    def _(i):
        hello(dev(y, lax.rem(z + i, NZ), k, c))

    @pl.loop(0, 8)
    def _(i):
        @pl.when(jnp.logical_not(on_diag & (i == me)))
        def _():
            hello(dev(i // 2, z, lax.rem(i, 2), y))

    loads[0].wait()
    target = hilbert[...]
    rel = jnp.where(target >= 0, (target >> 10) - c * 32, -1)
    hot = onehot(iota((32, 2048), 0) == rel)
    upper = onehot(iota((256, 256), 0) < iota((256, 256), 1))
    before = jnp.zeros((32, 1), f32)
    cell = jnp.zeros((512, 256), f32)
    for b in range(8):
        part = hot[:, b * 256:(b + 1) * 256]
        part32 = part.astype(f32)
        rank = jnp.sum((dot(part, upper) + before) * part32, axis=0, keepdims=True)
        before = before + jnp.sum(part32, axis=1, keepdims=True)
        r = rel[:, b * 256:(b + 1) * 256]
        index = jnp.where((r >= 0) & (r < 32), r * 16 + rank.astype(jnp.int32), -1)
        number = jnp.where(iota((256, 256), 1) >= 128, iota((256, 256), 0), b)
        cell = cell + dot(onehot(iota((512, 256), 0) == index), number.astype(f32).astype(BF16))
    cell = cell[:, :128] * 256.0 + cell[:, 128:]

    @pl.when(on_diag)
    def _():
        pl.semaphore_wait(barrier, 26)

    @pl.when(jnp.logical_not(on_diag))
    def _():
        pl.semaphore_wait(barrier, 27)

    def parts(a):
        return ((qkv_h, wq, 32, True), (fc1_h, w1, 128, False), (proj_h, wp, 32, False),
                (fc2_h, w2, 128, False))[a]

    def weight_x(a, i):
        src, dst, size, deep = parts(a)
        half = pl.ds(pl.multiple_of(k * size, size), size)
        return pltpu.make_async_remote_copy(
            src_ref=src.at[:, half] if deep else src.at[half],
            dst_ref=dst.at[c, :, half] if deep else dst.at[c, half],
            send_sem=ws.at[a, i], recv_sem=wr.at[a, i],
            device_id=dev(y, z, k, lax.rem(c + i, 4)), device_id_type=MESH)

    def weight_core(a, i):
        _, dst, size, deep = parts(a)
        half = pl.ds(pl.multiple_of(k * size, size), size)
        owner = lax.rem(c - i + 4, 4)
        at = dst.at[owner, :, half] if deep else dst.at[owner, half]
        return pltpu.make_async_remote_copy(
            src_ref=at, dst_ref=at, send_sem=fs.at[a, i], recv_sem=fr.at[a, i],
            device_id=dev(y, z, 1 - k, c), device_id_type=MESH)

    for i in range(1, 4):
        weight_x(0, i).start()

    loads[2].wait()
    loads[3].wait()
    total = jnp.zeros((512, 256), f32)
    one = jnp.ones((512, 128), BF16)
    points = ids[...].astype(f32)
    for b in range(6):
        member = jnp.concatenate(
            [onehot(cell == points[4 * b + j:4 * b + j + 1]) for j in range(4)], axis=1)
        total = total + dot(member, jnp.concatenate([raw[b * 512:(b + 1) * 512], one], axis=1))
    mean = (total[:, :128] / total[:, 128:]).astype(BF16)
    for zz in range(NZ):
        for kk in range(2):
            slots[zz, kk] = mean[zz * 32 + kk * 16:zz * 32 + kk * 16 + 16]

    def rows_z(j):
        zz = lax.rem(z + hop(j), NZ)
        return pltpu.make_async_remote_copy(
            src_ref=slots.at[zz], dst_ref=mid.at[j], send_sem=s2.at[j], recv_sem=r2.at[j],
            device_id=dev(y, zz, k, c), device_id_type=MESH)

    @pl.loop(1, NZ)
    def _(j):
        rows_z(NZ - j).start()
    own_z = pltpu.make_async_copy(slots.at[z], mid.at[0], r2.at[0])
    own_z.start()

    def is_me(i):
        return on_diag & (i == c * 2 + k)

    def on(g, i):
        kk, cc = lax.rem(i, 2), i // 2
        return pltpu.make_async_remote_copy(
            src_ref=mid.at[4 * g:4 * g + 4, kk], dst_ref=rows.at[4 * g:4 * g + 4, me],
            send_sem=s3.at[g, i], recv_sem=r3.at[g, me],
            device_id=dev(c, z, kk, cc), device_id_type=MESH)

    def on_start(g):
        @pl.loop(0, 8)
        def _(i):
            @pl.when(is_me(i))
            def _():
                pltpu.make_async_copy(mid.at[4 * g:4 * g + 4, k], rows.at[4 * g:4 * g + 4, me],
                                      r3.at[g, me]).start()

            @pl.when(jnp.logical_not(is_me(i)))
            def _():
                on(g, i).start()

    def on_arrived(g):
        @pl.loop(0, 8)
        def _(i):
            block = rows.at[4 * g:4 * g + 4, i]
            pltpu.make_async_copy(block, block, r3.at[g, i]).wait()

    loads[1].wait()
    z_rows = zpos[...]
    z32 = z_rows.astype(f32)
    column = jnp.concatenate(
        [jnp.transpose(jnp.broadcast_to(z32[j:j + 1], (128, 128))) for j in range(8)], axis=0)
    split = jnp.zeros((32, 128), f32)
    for j in range(8):
        rank = jnp.sum(jnp.where(column < z32[j:j + 1], 1.0, 0.0), axis=0, keepdims=True)
        rank = rank.astype(jnp.int32)
        own = z_rows[j:j + 1] & 1023
        dest = rank >> 3
        lane = ((dest >> 5) * 2 + (dest & 1)) * 8 + (rank & 7)
        sub = iota((32, 128), 0)
        digit = jnp.where(sub < 16, own >> 5, own & 31).astype(f32)
        left = jnp.where((sub & 15) == ((dest >> 1) & 15), digit, 0.0).astype(BF16)
        split = split + dot_nt(left, onehot(iota((128, 128), 0) == lane))
    table = (split[:16] * 32.0 + split[16:]).astype(jnp.int32)
    for zz in range(NZ):
        pos[zz] = table[zz:zz + 1]

    def pos_z(j):
        zz = lax.rem(z + j, NZ)
        return pltpu.make_async_remote_copy(
            src_ref=pos.at[zz], dst_ref=posz.at[z], send_sem=ps.at[j], recv_sem=pr.at[j],
            device_id=dev(y, zz, k, c), device_id_type=MESH)

    def pos_arrived(j):
        zs = lax.rem(z - j + NZ, NZ)
        return pltpu.make_async_copy(posz.at[zs], posz.at[zs], pr.at[j])

    own_pos = pltpu.make_async_copy(pos.at[z], posz.at[z], pr.at[0])
    own_pos.start()

    loads[4].wait()
    units = jnp.broadcast_to((counts[...] >> 7).astype(f32).astype(BF16), (8, 128))
    col = iota((128, 2048), 1)
    hop_no, from_yc = col >> 7, (col >> 4) & 7
    away = jnp.where((hop_no & 1) == 1, (hop_no + 1) >> 1, NZ - (hop_no >> 1))
    source = (from_yc >> 1) * 32 + ((z + NZ - away) & 15) * 2 + (from_yc & 1)
    held = dot(units, onehot(iota((128, 2048), 0) == source))[:1].astype(jnp.int32)
    first = dot(units, onehot(iota((128, 2048), 0) < source))[:1].astype(jnp.int32)
    within = iota((1, 2048), 1) & 15
    order = jnp.where(within < held, first + within, -1)

    def gather_group(g):
        on_arrived(g)
        sel = onehot(iota((1024, 512), 0) == order[:, g * 512:(g + 1) * 512])
        piece = dot(sel, rows[4 * g:4 * g + 4].reshape(512, 128))
        if g == 0:
            acc[...] = piece
        else:
            acc[...] += piece

    for g in range(4):
        for j in range(4 * g, 4 * g + 4):
            pltpu.make_async_copy(mid.at[j], mid.at[j], r2.at[j]).wait()
        on_start(g)
        if g == 0:
            @pl.loop(1, NZ)
            def _(j):
                pos_z(j).start()
    for i in range(1, 4):
        weight_x(0, i).wait_recv()
        weight_core(0, i).start()
    for g in range(4):
        gather_group(g)
    for a in range(1, 4):
        for i in range(1, 4):
            weight_x(a, i).start()

    @pl.loop(0, NZ)
    def _(j):
        pos_arrived(j).wait()

    def pos_on(i):
        return pltpu.make_async_remote_copy(
            src_ref=posz, dst_ref=posall.at[me], send_sem=qs.at[i], recv_sem=qr.at[me],
            device_id=dev(c, z, lax.rem(i, 2), i // 2), device_id_type=MESH)

    @pl.loop(0, 8)
    def _(i):
        @pl.when(is_me(i))
        def _():
            pltpu.make_async_copy(posz, posall.at[me], qr.at[me]).start()

        @pl.when(jnp.logical_not(is_me(i)))
        def _():
            pos_on(i).start()

    x = acc[...].astype(BF16)
    loads[5].wait()
    w = pool[...]
    normed = row_norm(dot(x, w).astype(BF16).astype(f32))
    t = iota((256, 256), 0)
    hop_no = 15 - ((t >> 7) * 8 + ((t >> 2) & 7))
    away = jnp.where((hop_no & 1) == 1, (hop_no + 1) >> 1, NZ - (hop_no >> 1))
    row = 8 * (((z + away) & 15) * 2 + ((t >> 5) & 1)) + 4 * ((t >> 6) & 1) + (t & 3)
    quarter = acc[pl.ds(pl.multiple_of(c * 256, 256), 256)].astype(BF16)
    mine = dot(onehot(iota((256, 256), 1) == row), quarter)
    features = dot(mine.astype(BF16), w).astype(BF16).astype(f32)
    loads[6].wait()
    for i in range(1, 4):
        weight_core(0, i).wait_recv()
    keys = dot_nt(wq[:, 1].reshape(256, 256), normed).astype(BF16)
    values = dot_nt(normed, wq[:, 2].reshape(256, 256)).astype(BF16)
    query = dot_nt(row_norm(features), wq[:, 0].reshape(256, 256)).astype(BF16).astype(f32)
    head_of = iota((256, 256), 1) >> 4
    ones = jnp.ones((1024, 128), BF16)
    summed = [jnp.concatenate([values[:, u * 128:(u + 1) * 128], ones], axis=1) for u in range(2)]
    scale = 0.25 * 1.4426950408889634

    def score(h):
        return dot(jnp.where(head_of == h, query, 0.0).astype(BF16), keys)

    lane_head = iota((256, 128), 1) >> 4
    sides = [jnp.zeros((256, 128), f32)] * 2
    scores = score(0)
    for h in range(16):
        later = score(h + 1) if h < 15 else None
        if h == 14:
            for a in range(1, 4):
                for i in range(1, 4):
                    weight_x(a, i).wait_recv()
                    weight_core(a, i).start()
        peak = jnp.max(scores, axis=1, keepdims=True)
        mix = dot(jnp.exp2((scores - peak) * scale).astype(BF16), summed[h // 8])
        sides[h // 8] = jnp.where(lane_head == h % 8, mix[:, :128] / mix[:, 128:], sides[h // 8])
        scores = later
    attended = jnp.concatenate(sides, axis=1).astype(BF16)
    for load in loads[7:]:
        load.wait()
    for a in range(1, 4):
        for i in range(1, 4):
            weight_core(a, i).wait_recv()
    middle = (features + dot_nt(attended, wp[...].reshape(256, 256))).astype(BF16).astype(f32)

    def back_xy(q, i):
        kk, cc = lax.rem(i, 2), i // 2
        return pltpu.make_async_remote_copy(
            src_ref=out.at[q, kk, cc], dst_ref=mid2.at[q, me], send_sem=c1s.at[q, i], recv_sem=c1r.at[q, me],
            device_id=dev(c, z, kk, cc), device_id_type=MESH)

    def forward(q):
        part = middle[q * 128:(q + 1) * 128]
        normed2 = row_norm(part)
        for i in range(4):
            v = dot(normed2, w1[i])
            hidden = (v * (1.0 + lax.erf(v * 0.7071067811865476)) * 0.5).astype(BF16)
            part = part + dot(hidden, w2[i])
        for kk in range(2):
            for cc in range(4):
                both = [part[h * 64 + kk * 32:h * 64 + kk * 32 + 32, cc * 64:cc * 64 + 64] for h in range(2)]
                out[q, kk, cc] = jnp.concatenate(both, axis=1).reshape(8, 4, 128).astype(BF16)

        @pl.loop(0, 8)
        def _(i):
            @pl.when(is_me(i))
            def _():
                pltpu.make_async_copy(out.at[q, k, c], mid2.at[q, me], c1r.at[q, me]).start()

            @pl.when(jnp.logical_not(is_me(i)))
            def _():
                back_xy(q, i).start()

    def back_z(j):
        zz = lax.rem(z + hop(j), NZ)
        at = NZ - 1 - j
        return pltpu.make_async_remote_copy(
            src_ref=mid2.at[at // 8, :, lax.rem(at, 8)], dst_ref=back.at[z], send_sem=c2s.at[j],
            recv_sem=c2r.at[j], device_id=dev(y, zz, k, c), device_id_type=MESH)

    def middle_arrived(q):
        @pl.loop(0, 8)
        def _(i):
            pltpu.make_async_copy(mid2.at[q, i], mid2.at[q, i], c1r.at[q, i]).wait()

    forward(0)
    forward(1)
    middle_arrived(0)

    @pl.loop(0, 8)
    def _(i):
        back_z(NZ - 1 - i).start()

    @pl.loop(0, 8)
    def _(i):
        pltpu.make_async_copy(posall.at[i], posall.at[i], qr.at[i]).wait()
    table = posall[...].reshape(128, 128)
    pick = onehot(iota((8, 128), 1) == me * 8 + iota((8, 128), 0))
    digits = [dot_nt(pick, part.astype(f32).astype(BF16)).astype(BF16) for part in (table >> 5, table & 31)]
    n = iota((128, 512), 1)
    spread = onehot(iota((128, 512), 0) == ((n >> 2) & 7) * 16 + (n >> 5))
    full = dot(digits[0], spread) * 32.0 + dot(digits[1], spread)
    sub, lane = iota((8, 512), 0), iota((8, 512), 1)
    wants = []
    for h in range(2):
        want = jnp.sum(jnp.where(sub == h * 4 + (lane & 3), full, 0.0), axis=0, keepdims=True)
        wants.append(want.astype(jnp.int32))

    middle_arrived(1)

    @pl.loop(8, NZ - 1)
    def _(i):
        back_z(NZ - 1 - i).start()
    own_back = pltpu.make_async_copy(mid2.at[1, :, 7], back.at[z], c2r.at[0])
    own_back.start()
    for h in range(2):
        placing[h] = onehot(iota((1024, 512), 0) == wants[h])

    for a in range(4):
        for i in range(1, 4):
            weight_x(a, i).wait_send()
            weight_core(a, i).wait_send()

    @pl.loop(1, NZ)
    def _(j):
        rows_z(j).wait_send()
        pos_z(j).wait_send()

    @pl.loop(0, 8)
    def _(i):
        @pl.when(jnp.logical_not(is_me(i)))
        def _():
            pos_on(i).wait_send()
            back_xy(0, i).wait_send()
            back_xy(1, i).wait_send()
            for g in range(4):
                on(g, i).wait_send()
    own_back.wait()

    @pl.loop(1, NZ)
    def _(i):
        back_z(i).wait()
    got = jnp.transpose(back[...].astype(f32).reshape(512, 128)).astype(BF16)
    result_t[...] = (dot_nt(got[:64], placing[0]) + dot_nt(got[64:], placing[1])).astype(BF16)


def shards(raw_points, cell_ids, row_counts, hilbert_position, z_position,
           pool_weight, qkv_weight, proj_weight, fc1_weight, fc2_weight):
    S, V, I32 = jax.ShapeDtypeStruct, pltpu.VMEM, jnp.int32

    def sems(*shape):
        return pltpu.SemaphoreType.DMA(shape)
    out = pl.pallas_call(
        layer_kernel,
        out_shape=S((64, 1024), BF16),
        in_specs=[ANY] * 10,
        out_specs=VM,
        scratch_shapes=[
            V((3072, 128), BF16), V((24, 128), I32), V((1, 2048), I32), V((8, 128), I32), V((1, 128), I32),
            V((128, 256), BF16), V((4, 3, 64, 256), BF16), V((4, 64, 256), BF16), V((4, 256, 256), BF16),
            V((4, 256, 256), BF16),
            V((NZ, 2, 16, 128), BF16), V((NZ, 1, 128), I32), V((NZ, 1, 128), I32), V((8, NZ, 1, 128), I32),
            V((NZ, 2, 16, 128), BF16), V((NZ, 8, 16, 128), BF16), V((1024, 128), jnp.float32),
            V((2, 2, 4, 8, 4, 128), BF16), V((2, 8, 8, 4, 128), BF16),
            sems(10), sems(NZ), sems(NZ), sems(NZ), sems(NZ), sems(4, 8), sems(4, 8),
            sems(4, 4), sems(4, 4), sems(4, 4), sems(4, 4), sems(8), sems(8), sems(2, 8), sems(2, 8), sems(NZ), sems(NZ),
            V((NZ, 8, 4, 128), BF16), V((2, 1024, 512), BF16),
        ],
        compiler_params=pltpu.CompilerParams(collective_id=0, has_side_effects=True,
                                             vmem_limit_bytes=LIMIT),
        name="layer",
    )(raw_points, cell_ids.reshape(24, 128), hilbert_position, z_position.reshape(8, 128),
      row_counts.reshape(1, 128), pool_weight, jnp.transpose(qkv_weight, (0, 2, 1)), proj_weight.T,
      fc1_weight, fc2_weight)
    return out.T


def solution(mesh):
    in_specs = (P("pts", None), P("pts"), P(), P("pts", None), P("pts"), P(),
                P(None, None, "ch"), P(None, "ch"), P(None, "ch"), P("ch", None))
    return jax.shard_map(shards, mesh=mesh, in_specs=in_specs, out_specs=P("pts", "ch"),
                         check_vma=False)
```
